128 devices in a mesh: section: 4 (over z), seq: 32 (over x, y, core).
Axes of the slice: x: 4, y: 4, z: 4, core: 2. Of those that a mesh axis runs over, the one named last changes fastest.
Arguments:
- section_input: bfloat16 [4, 4096, 4096], P('section', 'seq'), may hold values from -54 to 54, as said below
- sent_grad: bfloat16 [4, 4096, 4096], P('section', 'seq'), may hold values from -6 to 6
- norm_gain: float32 [4, 4096], P('section'), may hold values from 0.1 to 1.9
- short_filter: float32 [4, 21, 4096], P('section'), may hold values from -3.3 to 3.3
- log_rate: float32 [4, 16, 256], P('section'), may hold values from -10 to -3.4, as said below
- residue: float32 [4, 16, 256], P('section'), may hold values from -1 to 1
- skip_gain: float32 [4, 4096], P('section'), may hold values from -1 to 1
Outputs:
- block_out: bfloat16 [4, 4096, 4096], P('section', 'seq')
- input_grad: bfloat16 [4, 4096, 4096], P('section', 'seq')
- channel_grads: float32 [4, 32, 23, 4096], P('section', 'seq')
- residue_grads: float32 [4, 32, 16, 256], P('section', 'seq')
- rate_grads: float32 [4, 32, 16, 256], P('section', 'seq')
The draws below stay inside these ranges and needn't reach their ends.
Inputs may be any that keep to these rules, and one draw needn't show every extreme that they name: `section_input`: row and channel scales of the inputs vary. log_rate and residue are drawn together.
All inputs are finite; a program needn't handle non-finite values.
Results may differ from the reference program's by a relative error of at most 0.0072.
Values may be sent and summed in bfloat16 or wider, within the bound.
No kernel may reach another device: no remote copies, remote signals or barrier semaphores. Data moves between devices by JAX's collectives and lax.ppermute only.
A program may use at most 320 MiB of HBM per device.

```python
import math
import jax
import jax.numpy as jnp
from jax import lax

D = 4096
NS = 16
GS = 16
TAPS = 7
TOK_DEV = 128
NGROUP = 256
TOKENS = 4096
N_SECTION = 4
N_SEQ = 32


def mode_table(key):
    base = jax.random.fold_in(key, 11)
    key_pick, key_slow, key_fast, key_sign, key_size = jax.random.split(base, 5)
    shape = (N_SECTION, NS, NGROUP)
    share = 0.6
    chosen = jax.random.uniform(key_pick, shape) < share
    slow_log = jax.random.uniform(key_slow, shape, minval=math.log(0.05 / TOK_DEV), maxval=math.log(0.095 / TOK_DEV))
    fast_log = jax.random.uniform(key_fast, shape, minval=math.log(0.1 / TOK_DEV), maxval=math.log(1.0 / 30.0))
    log_rate = jnp.where(chosen, slow_log, fast_log)
    decay_base = jnp.exp(-jnp.exp(log_rate))
    signs = jnp.where(jax.random.uniform(key_sign, shape) < 0.5, -1.0, 1.0)
    magnitude = jax.random.uniform(key_size, shape, minval=0.2, maxval=0.5)
    residue = signs * magnitude * jnp.sqrt(1.0 - decay_base * decay_base + 1.0 / TOKENS)
    return (log_rate.astype(jnp.float32), residue.astype(jnp.float32))


def draw_log_rate(key, part):
    return mode_table(key)[0]


def draw_residue(key, part):
    return mode_table(key)[1]


def draw_short_filter(key, part):
    key_query, key_key, key_value = jax.random.split(jax.random.fold_in(key, 7), 3)
    shape = (N_SECTION, TAPS, D)
    query_base = jnp.clip(jax.random.normal(key_query, shape), -6.0, 6.0)
    key_base = jnp.clip(jax.random.normal(key_key, shape), -6.0, 6.0)
    value_base = jnp.clip(jax.random.normal(key_value, shape), -6.0, 6.0)
    factor = 1.0 / math.sqrt(TAPS)
    paired = factor / math.sqrt(2.0)
    query_taps = query_base * factor
    key_taps = (key_base + key_base[:, ::-1]) * paired
    value_taps = (value_base - value_base[:, ::-1]) * paired
    return jnp.concatenate([query_taps, key_taps, value_taps], 1).astype(jnp.float32)


def draw_section_input(key, part):
    key_main, key_row, key_col = jax.random.split(jax.random.fold_in(key, 5), 3)
    shape = (N_SECTION, TOKENS, D)
    main = jnp.clip(jax.random.normal(key_main, shape), -6.0, 6.0)
    row_scale = jnp.exp(jax.random.uniform(key_row, (N_SECTION, TOKENS, 1), minval=math.log(0.3), maxval=math.log(3.0)))
    col_scale = jnp.exp(jax.random.uniform(key_col, (N_SECTION, 1, D), minval=math.log(0.3), maxval=math.log(3.0)))
    return (main * row_scale * col_scale).astype(jnp.bfloat16)


def block_levels(stream_key, shape, shards, low, top_value):
    def one(position, blocks):
        draws = jax.random.uniform(jax.random.fold_in(jax.random.fold_in(stream_key, 6), position), (blocks,), jnp.float32, low / len(shards), top_value / len(shards))
        return jnp.repeat(jnp.exp(draws), shape[position] // blocks).reshape((-1,) + (1,) * (len(shape) - position - 1))

    factor_of = one(*shards[0])
    for cut in shards[1:]:
        factor_of = factor_of * one(*cut)
    return factor_of


def centred(rng, shape, deviation, bound, cuts=(), dtype=jnp.bfloat16):
    values = deviation * jax.random.normal(rng, shape, jnp.float32)
    if cuts:
        values = values * block_levels(rng, shape, cuts, -0.22, 0.18)
    return jnp.clip(values, -bound, bound).astype(dtype)


def setup_inputs(seed: int = 0) -> dict:
    key_of = jax.random.split(jax.random.key(seed), 8)
    return {
        "section_input": draw_section_input(jax.random.fold_in(key_of[7], 71), 0),
        "sent_grad": centred(key_of[1], (N_SECTION, TOKENS, D), 1.0, 6.0, ((0, 4), (1, 32))),
        "norm_gain": jnp.clip(1.0 + 0.18 * jax.random.normal(key_of[2], (N_SECTION, D), jnp.float32), 0.1, 1.9),
        "short_filter": draw_short_filter(jax.random.fold_in(key_of[7], 71), 0),
        "log_rate": draw_log_rate(jax.random.fold_in(key_of[7], 71), 0),
        "residue": draw_residue(jax.random.fold_in(key_of[7], 71), 0),
        "skip_gain": jnp.clip(jax.random.uniform(key_of[6], (N_SECTION, D), jnp.float32, -1.0, 1.0) * block_levels(key_of[6], (N_SECTION, D), ((0, 4),), -0.4, 0.0), -1.0, 1.0),
    }


EPSILON = 1e-06

def one_section(inputs, arrived_raw, norm_gain, short_filter, log_rate, residue, skip_gain):
    token_count = inputs.shape[0]
    channels = inputs.shape[1]
    shard_count = N_SEQ
    xfloat = inputs.astype(jnp.float32)
    inverse = lax.rsqrt(lax.optimization_barrier(jnp.mean(xfloat * xfloat, axis=-1, keepdims=True)) + EPSILON)
    unscaled_normalized = xfloat * inverse
    rounded = lax.optimization_barrier((unscaled_normalized * norm_gain).astype(jnp.bfloat16))
    normed = rounded.astype(jnp.float32)
    front = jnp.concatenate([jnp.zeros((TAPS - 1, channels), jnp.float32), normed], 0)
    filters = short_filter.reshape(3, TAPS, channels)

    def feature(stream):
        return sum((filters[stream, offset] * front[TAPS - 1 - offset:TAPS - 1 - offset + token_count] for offset in range(TAPS)))
    query_rows = feature(0)
    key_rows = feature(1)
    value_rows = feature(2)
    product = key_rows * value_rows
    decay_rate = jnp.repeat(jnp.exp(log_rate), GS, axis=1)
    decay_base = jnp.exp(-decay_rate)
    weights = jnp.repeat(residue, GS, axis=1)
    product_shards = product.reshape(shard_count, TOK_DEV, channels)

    def forward_shard(start_state, rows_in):

        def advance(state, piece):
            state = decay_base * state + piece[None]
            return (state, lax.optimization_barrier(jnp.sum(weights * state, 0)))
        end_state, modal_rows = lax.scan(advance, start_state, rows_in)
        return (end_state, (modal_rows, start_state))
    _, (modal_rows, start_states) = lax.scan(forward_shard, jnp.zeros((NS, channels), jnp.float32), product_shards)
    modal_out = modal_rows.reshape(token_count, channels) + skip_gain * product
    block_out = (xfloat + query_rows * modal_out).astype(jnp.bfloat16)
    arrived = arrived_raw.astype(jnp.float32)
    grad_query = arrived * modal_out
    grad_modal = arrived * query_rows
    grad_shards = grad_modal.reshape(shard_count, TOK_DEV, channels)

    def backward_shard(adjoint_next, pieces):
        rows_in, grad_rows, start_state = pieces

        def forward_step(state, piece):
            state = decay_base * state + piece[None]
            return (state, state)
        _, states = lax.scan(forward_step, start_state, rows_in)
        previous = jnp.concatenate([start_state[None], states[:-1]], 0)

        def reverse_step(carried, items):
            adjoint, grad_res, grad_dec = carried
            grad_row, state_row, previous_row = items
            adjoint = weights * grad_row[None] + decay_base * adjoint
            grad_res = grad_res + grad_row[None] * state_row
            grad_dec = grad_dec + adjoint * previous_row
            return ((adjoint, grad_res, grad_dec), lax.optimization_barrier(jnp.sum(adjoint, 0)))
        zeros_state = jnp.zeros((NS, channels), jnp.float32)
        (adjoint_first, grad_res, grad_dec), adjoint_sum = lax.scan(reverse_step, (adjoint_next, zeros_state, zeros_state), (grad_rows, states, previous), reverse=True)
        return (adjoint_first, (adjoint_sum, grad_res, grad_dec))
    _, (adjoint_sum, grad_res, grad_dec) = lax.scan(backward_shard, jnp.zeros((NS, channels), jnp.float32), (product_shards, grad_shards, start_states), reverse=True)
    grad_product = adjoint_sum.reshape(token_count, channels) + skip_gain * grad_modal
    grad_key = grad_product * value_rows
    grad_value = grad_product * key_rows
    grad_residue = grad_res.reshape(shard_count, NS, NGROUP, GS).sum(-1)
    grad_rate = (grad_dec * (-decay_base * decay_rate)).reshape(shard_count, NS, NGROUP, GS).sum(-1)
    streams = [grad_query, grad_key, grad_value]
    backs = [jnp.concatenate([item, jnp.zeros((TAPS - 1, channels), jnp.float32)], 0) for item in streams]
    normalized_gradient = sum((filters[stream, offset] * backs[stream][offset:offset + token_count] for stream in range(3) for offset in range(TAPS)))
    filter_rows = []
    for stream in range(3):
        for offset in range(TAPS):
            term = streams[stream] * front[TAPS - 1 - offset:TAPS - 1 - offset + token_count]
            filter_rows.append(term.reshape(shard_count, TOK_DEV, channels).sum(1))
    gain_gradient = (normalized_gradient * unscaled_normalized).reshape(shard_count, TOK_DEV, channels).sum(1)
    grad_skip = (grad_modal * product).reshape(shard_count, TOK_DEV, channels).sum(1)
    channel_grads = jnp.stack(filter_rows + [gain_gradient, grad_skip], 1)
    scaled_result = normalized_gradient * norm_gain
    input_grad = arrived + inverse * (scaled_result - unscaled_normalized * lax.optimization_barrier(jnp.mean(scaled_result * unscaled_normalized, axis=-1, keepdims=True)))
    return (block_out, input_grad.astype(jnp.bfloat16), channel_grads, grad_residue, grad_rate)

def reference(section_input, sent_grad, norm_gain, short_filter, log_rate, residue, skip_gain):
    received = jnp.roll(sent_grad, -1, axis=0)

    def apply_section(pieces):
        return one_section(*pieces)
    results = lax.map(apply_section, (section_input, received, norm_gain, short_filter, log_rate, residue, skip_gain))
    return (results[0], results[1], results[2], results[3], results[4])
```

```python
import jax
import jax.numpy as jnp
from jax import lax
from jax.experimental import pallas as pl
from jax.experimental.pallas import tpu as pltpu
from jax.sharding import PartitionSpec as P

EPSILON = 1e-06
F32 = jnp.float32
BF16 = jnp.bfloat16
LANES = 128
STEP = 8
WIDE = STEP * LANES
BLOCK = 64
TABLE_STEP = 16
VMEM_LIMIT = 60 * 1024 * 1024


def iota(shape, axis):
    return lax.broadcasted_iota(jnp.int32, shape, axis)


def dot(a, b):
    return jnp.dot(a, b, preferred_element_type=F32)


def call(kernel, grid, ins, outs, scratch=(), micros=1.0, name=None):
    total = sum(a.size * a.dtype.itemsize for a, _, _ in ins)
    for shape, dtype, _, _ in outs:
        size = jnp.dtype(dtype).itemsize
        for n in shape:
            size *= n
        total += size
    return pl.pallas_call(
        kernel,
        grid=grid,
        in_specs=[pl.BlockSpec(b, m) for _, b, m in ins],
        out_specs=[pl.BlockSpec(b, m) for _, _, b, m in outs],
        out_shape=[jax.ShapeDtypeStruct(s, d) for s, d, _, _ in outs],
        scratch_shapes=list(scratch),
        compiler_params=pltpu.CompilerParams(
            dimension_semantics=("arbitrary",) * len(grid), vmem_limit_bytes=VMEM_LIMIT
        ),
        cost_estimate=pl.CostEstimate(
            flops=int(micros * 1.0e9),
            bytes_accessed=int(total) if micros else 0,
            transcendentals=0,
        ),
        name=name,
    )(*[a for a, _, _ in ins])


def lane_group(shape):
    return (iota(shape, 1) % LANES) // 16


def by_group(rows):
    own = lane_group(rows.shape)
    zero = jnp.zeros_like(rows)
    return jnp.concatenate([jnp.where(own == g, rows, zero) for g in range(8)], 0)


def own_group(rows):
    own = lane_group((16, rows.shape[1]))
    kept = rows[:16]
    for g in range(1, 8):
        kept = jnp.where(own == g, rows[16 * g : 16 * g + 16], kept)
    return kept


def side_by_side(rows):
    return jnp.concatenate([rows[:BLOCK], rows[BLOCK:]], 1)


def joined(first, rest, lanes):
    return jnp.concatenate([first[:, lanes], rest[:, lanes]], 0).astype(F32)


def stacked(rows):
    return jnp.concatenate([rows[:, :LANES], rows[:, LANES:]], 0)


def table_kernel(lr, w, lc, lrw, kk, r_e, w_e):
    shape = (16, LANES)
    first = iota(shape, 1) < BLOCK
    token = (iota(shape, 1) % BLOCK).astype(F32)
    own = lane_group(shape)

    def split(value):
        high = value.astype(BF16).astype(F32)
        return jnp.where(first, high, value - high)

    for c in range(lc.shape[0]):
        parts = [[] for _ in range(5)]
        rate_lanes = weight_lanes = None
        for g in range(8):
            at = c * 8 + g
            rate = jnp.broadcast_to(jnp.exp(lr[:, at : at + 1]), shape)
            weight = jnp.broadcast_to(w[:, at : at + 1], shape)
            end = jnp.exp(-rate * (BLOCK - 1.0 - token))
            start = jnp.exp(-rate * token)
            decay = jnp.exp(-rate)
            parts[0].append(split(end))
            parts[1].append(split((BLOCK - 1.0 - token) * end))
            parts[2].append(split(start))
            parts[3].append(split((token + 1.0) * start))
            parts[4].append(decay * jnp.where(first, weight * start, end))
            for i, value in enumerate((end, start)):
                row = jnp.sum(weight * value, axis=0, keepdims=True)
                kk[i, at : at + 1, :] = jnp.where(first[:1], row, 0.0)
            if g == 0:
                rate_lanes, weight_lanes = rate, weight
            else:
                rate_lanes = jnp.where(own == g, rate, rate_lanes)
                weight_lanes = jnp.where(own == g, weight, weight_lanes)
        for i in range(4):
            lc[c, i] = jnp.concatenate(parts[i], 0).astype(BF16)
        turned = jnp.concatenate(parts[4], 0).T.astype(BF16)
        lrw[c, 0] = turned[:BLOCK]
        lrw[c, 1] = turned[BLOCK:]
        lanes = slice(c * LANES, (c + 1) * LANES)
        r_e[:, lanes] = rate_lanes
        w_e[:, lanes] = weight_lanes


def features_kernel(
    x, xh, gain, filt, lc, kk, r_e, nrm, q, k, v, p, inside, inv_out, s, f, inv
):
    channels = x.shape[1]
    step = pl.program_id(0)

    @pl.when(step == 0)
    def _():
        def add(i, carry):
            own, halo = carry
            lanes = pl.ds(pl.multiple_of(i * LANES, LANES), LANES)
            a = x[:, lanes].astype(F32)
            b = xh[:, lanes].astype(F32)
            return own + a * a, halo + b * b

        own, halo = lax.fori_loop(
            0,
            channels // LANES,
            add,
            (jnp.zeros((LANES, LANES), F32), jnp.zeros((8, LANES), F32)),
            unroll=4,
        )
        for rows, total in ((slice(0, 8), halo), (slice(8, 136), own)):
            mean = jnp.sum(total, axis=1, keepdims=True) * (1.0 / channels)
            inverse = lax.rsqrt(mean + EPSILON)
            inv[rows, :] = jnp.broadcast_to(inverse, total.shape)
        inv_out[...] = inv[...]

    for c in range(STEP):
        local = slice(c * LANES, (c + 1) * LANES)
        lanes = pl.ds(pl.multiple_of((step * STEP + c) * LANES, LANES), LANES)
        gains = gain[:, local]
        own = x[:, lanes].astype(F32) * inv[8:136, :]
        nrm[c, 8:136, :] = (own * gains).astype(BF16).astype(F32)
        halo = xh[:, lanes].astype(F32) * inv[0:8, :]
        nrm[c, 0:8, :] = (halo * gains).astype(BF16).astype(F32)
        taps = [filt[j, 0:1, local] for j in range(21)]
        for r in range(0, LANES, 32):
            total = [jnp.zeros((32, LANES), F32) for _ in range(3)]
            for j in range(7):
                rows = nrm[c, 8 + r - j : 40 + r - j, :]
                for i in range(3):
                    total[i] = total[i] + taps[i * 7 + j] * rows
            q[c, r : r + 32, :] = total[0]
            k[c, r : r + 32, :] = total[1]
            v[c, r : r + 32, :] = total[2]
            product = total[1] * total[2]
            high = product.astype(BF16)
            p[0, c, r : r + 32, :] = high
            p[1, c, r : r + 32, :] = (product - high.astype(F32)).astype(BF16)
    for c in range(STEP):
        local = slice(c * LANES, (c + 1) * LANES)
        high, low = side_by_side(p[0, c]), side_by_side(p[1, c])
        table = lc[c].reshape(2 * LANES, LANES)
        sums = dot(
            jnp.concatenate([table, table], 1), jnp.concatenate([high, high, low, low], 0)
        )
        ends, ramps = own_group(sums[:LANES]), own_group(sums[LANES:])
        span = jnp.exp(-float(BLOCK) * r_e[:, local])
        s[:, local] = span * ends[:, :LANES] + ends[:, LANES:]
        f[0:32, local] = stacked(ends)
        f[32:64, local] = stacked(ramps)
        inside[c] = forward_blocks(p[0, c], kk[0, c * 8 : c * 8 + 8, :])


def forward_blocks(p, kernel):
    first = iota((BLOCK, LANES), 1) < BLOCK
    tiles = []
    for g in range(0, 8, 2):
        even, odd = (jnp.broadcast_to(kernel[i : i + 1], (BLOCK, LANES)) for i in (g, g + 1))
        even = pltpu.roll(even, BLOCK + 1, 1, stride=1, stride_axis=0)
        odd = pltpu.roll(odd, 1, 1, stride=1, stride_axis=0)
        tiles.append(jnp.where(first, even, odd).astype(BF16))
    return stacked(dot(jnp.concatenate(tiles, 1), by_group(side_by_side(p))))


def taken(grads, c, streams, taps, first, rows):
    total = None
    for i, stream in enumerate(streams):
        for j in range(7):
            term = taps[stream * 7 + j] * grads[c, i, first + j : first + j + rows, :]
            total = term if total is None else total + term
    return total


def tap_gradients(grads, nrm, c, count):
    sums = [jnp.zeros((8, LANES), F32) for _ in range(7 * count)]
    for r in range(0, LANES, 32):
        items = [grads[c, i, 8 + r : 40 + r, :] for i in range(count)]
        for j in range(7):
            rows = nrm[c, 8 + r - j : 40 + r - j, :]
            for i in range(count):
                term = (items[i] * rows).reshape(4, 8, LANES)
                sums[i * 7 + j] = sums[i * 7 + j] + jnp.sum(term, axis=0)
    return [jnp.sum(item, axis=0, keepdims=True) for item in sums]


def clear_ends(grads, count):
    @pl.when(pl.program_id(0) == 0)
    def _():
        for i in range(count):
            grads[:, i, 0:8, :] = jnp.zeros((STEP, 8, LANES), F32)
            grads[:, i, 136:144, :] = jnp.zeros((STEP, 8, LANES), F32)


def output_kernel(
    inside, lrw, e, f, r_e, q, k, v, x, skip, g, g_rest, nrm, filt, out, gn, fg, grads
):
    clear_ends(grads, 1)
    for c in range(STEP):
        local = slice(c * LANES, (c + 1) * LANES)
        state = e[:, local]
        second = f[:, local] + jnp.exp(-float(BLOCK) * r_e[:, local]) * state
        states = jnp.concatenate([state, second], 1).astype(BF16)
        carried = stacked(dot(lrw[c, 0], by_group(states)))
        product = k[c] * v[c]
        modal = inside[c] + carried + skip[:, local] * product
        query = q[c]
        arrived = joined(g, g_rest, local)
        out[:, local] = (x[:, local].astype(F32) + query * modal).astype(BF16)
        grads[c, 0, 8:136, :] = arrived * modal
        skip_grad = jnp.sum(arrived * query * product, axis=0, keepdims=True)
        taps = [filt[j, 0:1, local] for j in range(7)]
        gn[c, 0:8, :] = taken(grads, c, (0,), taps, 0, 8)
        for r in range(8, 136, 32):
            gn[c, r : r + 32, :] = taken(grads, c, (0,), taps, r, 32)
        fg[:, local] = jnp.concatenate(tap_gradients(grads, nrm, c, 1) + [skip_grad], 0)


def adjoint_kernel(g, g_rest, q, lc, w_e, r_e, gm, a, b):
    for c in range(STEP):
        local = slice(c * LANES, (c + 1) * LANES)
        grad = (joined(g, g_rest, local) * q[c]).astype(BF16)
        gm[c] = grad
        sides = side_by_side(grad)
        sums = dot(lc[c].reshape(2 * LANES, LANES), jnp.concatenate([sides, sides], 0))
        starts, ramps = own_group(sums[:LANES]), own_group(sums[LANES:])
        span = jnp.exp(-float(BLOCK) * r_e[:, local])
        first = w_e[:, local] * (starts[:, :LANES] + span * starts[:, LANES:])
        a[:, local] = first.astype(BF16)
        b[0:32, local] = stacked(starts)
        b[32:64, local] = stacked(ramps)


def backward_kernel(p, gm, kk, back, by_lag):
    first = iota((BLOCK, LANES), 1) < BLOCK
    both = iota((LANES, LANES), 0) + iota((LANES, LANES), 1)
    same = iota((LANES, LANES), 0) // BLOCK == iota((LANES, LANES), 1) // BLOCK
    flip = (same & (both % BLOCK == BLOCK - 1)).astype(BF16)
    for c in range(STEP):
        grads = by_group(side_by_side(gm[c]))
        tiles = []
        for g in range(0, 8, 2):
            even, odd = (
                jnp.broadcast_to(kk[0, c * 8 + i : c * 8 + i + 1, :], (BLOCK, LANES))
                for i in (g, g + 1)
            )
            even = pltpu.roll(even, 0, 1, stride=1, stride_axis=0)
            odd = pltpu.roll(odd, BLOCK, 1, stride=1, stride_axis=0)
            tiles.append(jnp.where(first, even, odd).astype(BF16))
        back[c] = stacked(dot(jnp.concatenate(tiles, 1), grads))
        sides = jnp.concatenate([side_by_side(p[0, c]), side_by_side(p[1, c])], 0)
        sides = dot(flip, sides).astype(BF16)
        crossed = lax.dot_general(
            sides, grads, (((1,), (1,)), ((), ())), preferred_element_type=F32
        )
        crossed = crossed[:BLOCK] + crossed[BLOCK:]
        for g in range(8):
            tile = crossed[:, g // 2 * LANES : (g // 2 + 1) * LANES]
            tile = jnp.where(first if g % 2 == 0 else ~first, tile, 0.0)
            tile = pltpu.roll(tile, g % 2 * BLOCK, 1, stride=1, stride_axis=0)
            by_lag[c * 8 + g : c * 8 + g + 1, :] = jnp.sum(tile, axis=0, keepdims=True)


def mixer_kernel(
    back, lrw, a, b, w_e, r_e, g, g_rest, q, k, v, gn0, nrm, filt, skip, gain, x, inv,
    gn, fg, hx, part, grads,
):
    clear_ends(grads, 2)

    @pl.when(pl.program_id(0) == 0)
    def _():
        hx[...] = jnp.zeros_like(hx)

    for c in range(STEP):
        local = slice(c * LANES, (c + 1) * LANES)
        second = a[:, local].astype(F32)
        span = jnp.exp(-float(BLOCK) * r_e[:, local])
        first = w_e[:, local] * b[:, local] + span * second
        states = jnp.concatenate([first, second], 1).astype(BF16)
        carried = stacked(dot(lrw[c, 0], by_group(states)))
        modal = joined(g, g_rest, local) * q[c]
        product = back[c] + carried + skip[:, local] * modal
        grads[c, 0, 8:136, :] = product * v[c]
        grads[c, 1, 8:136, :] = product * k[c]
        gains = gain[:, local]
        taps = [filt[j, 0:1, local] for j in range(21)]
        part[:, local] = (gn0[c, 0:8, :] + taken(grads, c, (1, 2), taps, 0, 8)).astype(BF16)
        gain_grad = jnp.zeros((8, LANES), F32)
        for r in range(0, LANES, 32):
            total = gn0[c, 8 + r : 40 + r, :] + taken(grads, c, (1, 2), taps, 8 + r, 32)
            gn[c, r : r + 32, :] = total
            xhat = x[r : r + 32, local].astype(F32) * inv[8 + r : 40 + r, :]
            both = total * xhat
            gain_grad = gain_grad + jnp.sum(both.reshape(4, 8, LANES), axis=0)
            hx[r : r + 32, :] += both * gains
        gain_grad = jnp.sum(gain_grad, axis=0, keepdims=True)
        rows = tap_gradients(grads, nrm, c, 2) + [gain_grad, jnp.zeros((1, LANES), F32)]
        fg[:, local] = jnp.concatenate(rows, 0)


def final_kernel(
    gn, g, g_rest, fg0, fg, hx, part, x, x_last, inv, gain, gain_all, out, cg, mean
):
    channels = x_last.shape[1]
    step = pl.program_id(0)

    @pl.when(step == 0)
    def _():
        def add(i, total):
            lanes = pl.ds(pl.multiple_of(i * LANES, LANES), LANES)
            xhat = x_last[8:16, lanes].astype(F32) * inv[128:136, :]
            return total + part[:, lanes].astype(F32) * gain_all[:, lanes] * xhat

        extra = lax.fori_loop(
            0, channels // LANES, add, jnp.zeros((8, LANES), F32), unroll=4
        )
        total = jnp.concatenate([hx[:120], hx[120:] + extra], 0)
        total = jnp.sum(total, axis=1, keepdims=True) * (1.0 / channels)
        mean[...] = jnp.broadcast_to(total, mean.shape)

    for c in range(STEP):
        local = slice(c * LANES, (c + 1) * LANES)
        lanes = pl.ds(pl.multiple_of((step * STEP + c) * LANES, LANES), LANES)
        arrived = joined(g, g_rest, local)
        extra = part[:, lanes].astype(F32)
        own = gn[c]
        own = jnp.concatenate([own[:120], own[120:] + extra], 0)
        xhat = x[:, local].astype(F32) * inv[8:136, :]
        result = arrived + inv[8:136, :] * (own * gain[:, local] - xhat * mean[...])
        out[:, local] = result.astype(BF16)
        fixed = jnp.sum(extra * xhat[120:], axis=0, keepdims=True)
        sources = [fg0[i : i + 1, local] for i in range(7)]
        sources += [fg[i : i + 1, local] for i in range(14)]
        sources += [fg[14:15, local] + fixed, fg0[7:8, local]]
        for i, source in enumerate(sources):
            cg[i, 0:1, local] = source


def modes_kernel(a, b, e, f, r_e, w_e, by_lag, lr, w, residue_out, rate_out):
    groups = lr.shape[1]
    chunks = e.shape[1] // LANES

    def chunk(i, total):
        lanes = pl.ds(pl.multiple_of(i * LANES, LANES), LANES)
        rate = r_e[:, lanes]
        weight = w_e[:, lanes]
        span = jnp.exp(-float(BLOCK) * rate)
        state0 = e[:, lanes]
        state1 = f[0:16, lanes] + span * state0
        adjoint1 = a[:, lanes].astype(F32)
        adjoint0 = weight * b[16:32, lanes] + span * adjoint1
        one = (state0 * b[0:16, lanes] + state1 * b[16:32, lanes]) * jnp.exp(-rate)
        two = weight * (state0 * b[32:48, lanes] + state1 * b[48:64, lanes])
        two = two + adjoint0 * f[32:48, lanes] + adjoint1 * f[48:64, lanes]
        two = two + BLOCK * span * (adjoint0 * state0 + adjoint1 * state1)
        both = jnp.concatenate([one, two], 0)
        high = both.astype(BF16)
        low = (both - high.astype(F32)).astype(BF16)
        shape = (LANES, groups)
        hot = (iota(shape, 1) == i * 8 + iota(shape, 0) // 16).astype(BF16)
        return total + dot(jnp.concatenate([high, low], 0), hot)

    totals = lax.fori_loop(0, chunks, chunk, jnp.zeros((64, groups), F32), unroll=8)
    totals = totals[:32] + totals[32:]
    lag = (iota((LANES, groups), 0) - (BLOCK - 1)).astype(F32)
    lags = jnp.where(lag >= 0.0, by_lag[...].T, 0.0)
    lag = jnp.maximum(lag, 0.0)
    for m in range(16):
        rate = jnp.exp(lr[m : m + 1, :])
        terms = jnp.exp(-rate * lag) * lags
        first = jnp.sum(terms, axis=0, keepdims=True)
        second = jnp.sum(terms * lag, axis=0, keepdims=True) * jnp.exp(rate)
        residue_out[m : m + 1, :] = first + totals[m : m + 1, :]
        decay = w[m : m + 1, :] * second + totals[16 + m : 17 + m, :]
        rate_out[m : m + 1, :] = decay * (-jnp.exp(-rate) * rate)


def levels_of(count):
    levels = []
    stride = 1
    while stride < count:
        size = 2 if stride == 1 else min(4, count // stride)
        levels.append((stride, size))
        stride *= size
    return levels


def after(value, *others):
    return lax.optimization_barrier((value, *others))[0]


class Prefix:
    def __init__(self, local, rate, rows, reverse):
        self.count = lax.axis_size("seq")
        self.mine = lax.axis_index("seq")
        self.local, self.rate, self.rows, self.reverse = local, rate, rows, reverse
        half = local.shape[1] // 2
        self.even = self.mine % 2 == 0
        self.half_rate = jnp.where(self.even, rate[:, :half], rate[:, half:])
        self.value = local
        self.levels = levels_of(self.count)
        self.above = 0.0
        self.low = 0.0

    def send(self, number):
        stride, size = self.levels[number]
        last = stride * size == self.count
        sign = -1 if self.reverse else 1
        self.got = []
        for h in range(1, size):
            pairs = []
            for i in range(self.count):
                there = (i // stride) % size + sign * h
                if last and not 0 <= there < size:
                    continue
                pairs.append((i, i + (there % size - (i // stride) % size) * stride))
            self.got.append(lax.ppermute(self.value, "seq", pairs))

    def join(self, number, *others):
        stride, size = self.levels[number]
        last = stride * size == self.count
        rate = self.rate if number == 0 else self.half_rate
        span = float(self.rows * stride)
        digit = (self.mine // stride) % size
        place = size - 1 - digit if self.reverse else digit
        got = self.got
        if others:
            got = [after(item, *others) for item in got]
        own = self.value.astype(F32)
        group = own * jnp.exp(-rate * (span * (size - 1 - place).astype(F32)))
        before = jnp.zeros_like(own)
        for h in range(1, size):
            item = got[h - 1].astype(F32)
            earlier = jnp.where(h <= place, 1.0, 0.0)
            before = before + item * (earlier * jnp.exp(-rate * (span * (h - 1))))
            if not last:
                away = (h - 1 - place) % size
                group = group + item * jnp.exp(-rate * (span * away.astype(F32)))
        if number == 0:
            self.near, self.place = before, place
            half = group.shape[1] // 2
            group = jnp.where(self.even, group[:, :half], group[:, half:])
        else:
            self.above = self.above + before * jnp.exp(-rate * (self.rows * self.low))
            self.low = self.low + (place * stride).astype(F32)
        self.value = group.astype(self.local.dtype)

    def swap(self):
        mine = self.above.astype(self.local.dtype)
        other = lax.ppermute(mine, "seq", [(i, i ^ 1) for i in range(self.count)])
        low = jnp.where(self.even, mine, other)
        high = jnp.where(self.even, other, mine)
        above = jnp.concatenate([low, high], 1).astype(F32)
        result = self.near + above * jnp.exp(
            -self.rate * (self.rows * self.place.astype(F32))
        )
        return result.astype(self.local.dtype)


def on_device(section_input, sent_grad, norm_gain, short_filter, log_rate, residue, skip_gain):
    x = section_input[0]
    rows, channels = x.shape
    groups = log_rate.shape[2]
    chunks = channels // LANES
    sections = lax.axis_size("section")
    count = lax.axis_size("seq")
    filt, gain, skip = short_filter.reshape(-1, 1, channels), norm_gain, skip_gain
    lr, w = log_rate[0], residue[0]

    ring = [(i, (i - 1) % sections) for i in range(sections)]
    cut = rows * 5 // 8
    g = lax.ppermute(sent_grad[0, :cut], "section", ring)
    g_rest = lax.ppermute(sent_grad[0, cut:], "section", ring)
    halo = lax.ppermute(x[rows - 8 :], "seq", [(i, i + 1) for i in range(count - 1)])

    full = lambda i: (0, 0)
    lane = lambda i: (0, i)
    block = lambda i: (i, 0, 0)
    cube = (STEP, LANES, LANES)
    tall = (STEP, LANES + 8, LANES)
    grid = (chunks // STEP,)
    table_step = min(TABLE_STEP, chunks)
    table_groups = 8 * table_step
    lc, lrw, kk, r_e, w_e = call(
        table_kernel,
        (chunks // table_step,),
        [(lr, (16, table_groups), lane), (w, (16, table_groups), lane)],
        [
            (
                (chunks, 4, LANES, LANES),
                BF16,
                (table_step, 4, LANES, LANES),
                lambda i: (i, 0, 0, 0),
            ),
            (
                (chunks, 2, BLOCK, LANES),
                BF16,
                (table_step, 2, BLOCK, LANES),
                lambda i: (i, 0, 0, 0),
            ),
            ((2, groups, LANES), F32, (2, table_groups, LANES), lambda i: (0, i, 0)),
            ((16, channels), F32, (16, table_step * LANES), lane),
            ((16, channels), F32, (16, table_step * LANES), lane),
        ],
        micros=0,
        name="tables",
    )
    wide16 = (16, WIDE)
    nrm, q, k, v, p, inside, inv, s, f = call(
        features_kernel,
        grid,
        [
            (x, (rows, channels), full),
            (halo, (8, channels), full),
            (gain, (1, WIDE), lane),
            (filt, (21, 1, WIDE), lambda i: (0, 0, i)),
            (lc, (STEP, 2, LANES, LANES), lambda i: (i, 0, 0, 0)),
            (kk, (1, 8 * STEP, LANES), lambda i: (0, i, 0)),
            (r_e, wide16, lane),
        ],
        [
            ((chunks, LANES + 8, LANES), F32, tall, block),
            ((chunks, LANES, LANES), F32, cube, block),
            ((chunks, LANES, LANES), F32, cube, block),
            ((chunks, LANES, LANES), F32, cube, block),
            ((2, chunks, LANES, LANES), BF16, (2,) + cube, lambda i: (0, i, 0, 0)),
            ((chunks, LANES, LANES), F32, cube, block),
            ((LANES + 8, LANES), F32, (LANES + 8, LANES), full),
            ((16, channels), F32, wide16, lane),
            ((64, channels), F32, (64, WIDE), lane),
        ],
        scratch=[pltpu.VMEM((LANES + 8, LANES), F32)],
        micros=0,
        name="features",
    )
    ahead = Prefix(after(s, g), r_e, rows, False)
    ahead.send(0)
    ahead.join(0)
    ahead.send(1)
    q_late = after(q, ahead.value)
    gm, a_local, b = call(
        adjoint_kernel,
        grid,
        [
            (g, (cut, WIDE), lane),
            (g_rest, (rows - cut, WIDE), lane),
            (q_late, cube, block),
            (lc, (STEP, 2, LANES, LANES), lambda i: (i, 1, 0, 0)),
            (w_e, wide16, lane),
            (r_e, wide16, lane),
        ],
        [
            ((chunks, LANES, LANES), BF16, cube, block),
            ((16, channels), BF16, wide16, lane),
            ((64, channels), F32, (64, WIDE), lane),
        ],
        micros=3,
        name="adjoint",
    )
    behind = Prefix(a_local, r_e, rows, True)
    behind.send(0)
    ahead.join(1, a_local)
    ahead.send(2)
    behind.join(0)
    behind.send(1)
    gm_late = after(gm, behind.value, ahead.value)
    back, by_lag = call(
        backward_kernel,
        grid,
        [
            (p, (2,) + cube, lambda i: (0, i, 0, 0)),
            (gm_late, cube, block),
            (kk, (1, 8 * STEP, LANES), lambda i: (1, i, 0)),
        ],
        [
            ((chunks, LANES, LANES), F32, cube, block),
            ((groups, LANES), F32, (8 * STEP, LANES), lambda i: (i, 0)),
        ],
        micros=6,
        name="backward",
    )
    behind.join(1, by_lag)
    behind.send(2)
    ahead.join(2, by_lag)
    e = after(ahead.swap(), behind.value)
    block_out, gn0, fg0 = call(
        output_kernel,
        grid,
        [
            (inside, cube, block),
            (lrw, (STEP, 1, BLOCK, LANES), lambda i: (i, 0, 0, 0)),
            (e, wide16, lane),
            (f, wide16, lane),
            (r_e, wide16, lane),
            (q, cube, block),
            (k, cube, block),
            (v, cube, block),
            (x, (rows, WIDE), lane),
            (skip, (1, WIDE), lane),
            (g, (cut, WIDE), lane),
            (g_rest, (rows - cut, WIDE), lane),
            (nrm, tall, block),
            (filt, (21, 1, WIDE), lambda i: (0, 0, i)),
        ],
        [
            ((rows, channels), BF16, (rows, WIDE), lane),
            ((chunks, LANES + 8, LANES), F32, tall, block),
            ((8, channels), F32, (8, WIDE), lane),
        ],
        scratch=[pltpu.VMEM((STEP, 1, LANES + 16, LANES), F32)],
        micros=8,
        name="output",
    )
    behind.join(2, fg0)
    a = behind.swap()
    gn, fg, hx, part = call(
        mixer_kernel,
        grid,
        [
            (back, cube, block),
            (lrw, (STEP, 1, BLOCK, LANES), lambda i: (i, 1, 0, 0)),
            (a, wide16, lane),
            (b, wide16, lambda i: (1, i)),
            (w_e, wide16, lane),
            (r_e, wide16, lane),
            (g, (cut, WIDE), lane),
            (g_rest, (rows - cut, WIDE), lane),
            (q, cube, block),
            (k, cube, block),
            (v, cube, block),
            (gn0, tall, block),
            (nrm, tall, block),
            (filt, (21, 1, WIDE), lambda i: (0, 0, i)),
            (skip, (1, WIDE), lane),
            (gain, (1, WIDE), lane),
            (x, (rows, WIDE), lane),
            (inv, (LANES + 8, LANES), full),
        ],
        [
            ((chunks, LANES, LANES), F32, cube, block),
            ((16, channels), F32, wide16, lane),
            ((LANES, LANES), F32, (LANES, LANES), full),
            ((8, channels), BF16, (8, WIDE), lane),
        ],
        scratch=[pltpu.VMEM((STEP, 2, LANES + 16, LANES), F32)],
        micros=10,
        name="mixer",
    )
    part = lax.ppermute(part, "seq", [(i + 1, i) for i in range(count - 1)])
    whole = lambda value: (value, value.shape, lambda i: (0,) * value.ndim)
    residue_grads, rate_grads = call(
        modes_kernel,
        (1,),
        [whole(value) for value in (a, b, e, f, r_e, w_e, by_lag, lr, w)],
        [((16, groups), F32, (16, groups), full)] * 2,
        micros=3,
        name="modes",
    )
    input_grad, channel_grads = call(
        final_kernel,
        grid,
        [
            (gn, cube, block),
            (g, (cut, WIDE), lane),
            (g_rest, (rows - cut, WIDE), lane),
            (fg0, (8, WIDE), lane),
            (fg, wide16, lane),
            (hx, (LANES, LANES), full),
            (part, (8, channels), full),
            (x, (rows, WIDE), lane),
            (x, (16, channels), lambda i: (rows // 16 - 1, 0)),
            (inv, (LANES + 8, LANES), full),
            (gain, (1, WIDE), lane),
            (gain, (1, channels), full),
        ],
        [
            ((rows, channels), BF16, (rows, WIDE), lane),
            ((23, 1, channels), F32, (23, 1, WIDE), lambda i: (0, 0, i)),
        ],
        scratch=[pltpu.VMEM((LANES, LANES), F32)],
        micros=4,
        name="final",
    )
    return (
        block_out[None],
        input_grad[None],
        channel_grads.reshape(1, 1, 23, channels),
        residue_grads[None, None],
        rate_grads[None, None],
    )


def solution(mesh):
    placed = (
        P("section", "seq", None),
        P("section", "seq", None),
        P("section", None),
        P("section", None, None),
        P("section", None, None),
        P("section", None, None),
        P("section", None),
    )
    return jax.shard_map(
        on_device,
        mesh=mesh,
        in_specs=placed,
        out_specs=(
            P("section", "seq", None),
            P("section", "seq", None),
            P("section", "seq", None, None),
            P("section", "seq", None, None),
            P("section", "seq", None, None),
        ),
        check_vma=False,
    )
```

```python
import jax
import jax.numpy as jnp
from jax import lax
from jax.experimental import pallas as pl
from jax.experimental.pallas import tpu as pltpu
from jax.sharding import PartitionSpec as P

EPSILON = 1e-06
F32 = jnp.float32
BF16 = jnp.bfloat16
LANES = 128
STEP = 8
WIDE = STEP * LANES
BLOCK = 64
TABLE_STEP = 16
VMEM_LIMIT = 20 * 1024 * 1024


def iota(shape, axis):
    return lax.broadcasted_iota(jnp.int32, shape, axis)


def dot(a, b):
    return jnp.dot(a, b, preferred_element_type=F32)


def call(kernel, grid, ins, outs, scratch=(), micros=1.0, name=None):
    total = sum(a.size * a.dtype.itemsize for a, _, _ in ins)
    for shape, dtype, _, _ in outs:
        size = jnp.dtype(dtype).itemsize
        for n in shape:
            size *= n
        total += size
    return pl.pallas_call(
        kernel,
        grid=grid,
        in_specs=[pl.BlockSpec(b, m) for _, b, m in ins],
        out_specs=[pl.BlockSpec(b, m) for _, _, b, m in outs],
        out_shape=[jax.ShapeDtypeStruct(s, d) for s, d, _, _ in outs],
        scratch_shapes=list(scratch),
        compiler_params=pltpu.CompilerParams(
            dimension_semantics=("arbitrary",) * len(grid), vmem_limit_bytes=VMEM_LIMIT
        ),
        cost_estimate=pl.CostEstimate(
            flops=int(micros * 1.0e9),
            bytes_accessed=int(total) if micros else 0,
            transcendentals=0,
        ),
        name=name,
    )(*[a for a, _, _ in ins])


def lane_group(shape):
    return (iota(shape, 1) % LANES) // 16


def by_group(rows):
    own = lane_group(rows.shape)
    zero = jnp.zeros_like(rows)
    return jnp.concatenate([jnp.where(own == g, rows, zero) for g in range(8)], 0)


def own_group(rows):
    own = lane_group((16, rows.shape[1]))
    kept = rows[:16]
    for g in range(1, 8):
        kept = jnp.where(own == g, rows[16 * g : 16 * g + 16], kept)
    return kept


def side_by_side(rows):
    return jnp.concatenate([rows[:BLOCK], rows[BLOCK:]], 1)


def joined(parts, lanes):
    return jnp.concatenate([part[:, lanes] for part in parts], 0).astype(F32)


def stacked(rows):
    return jnp.concatenate([rows[:, :LANES], rows[:, LANES:]], 0)


def table_kernel(lr, w, lc, lrw, kk, r_e, w_e):
    shape = (16, LANES)
    first = iota(shape, 1) < BLOCK
    token = (iota(shape, 1) % BLOCK).astype(F32)
    own = lane_group(shape)

    def split(value):
        high = value.astype(BF16).astype(F32)
        return jnp.where(first, high, value - high)

    for c in range(lc.shape[0]):
        parts = [[] for _ in range(4)]
        rate_lanes = weight_lanes = None
        for g in range(8):
            at = c * 8 + g
            rate = jnp.broadcast_to(jnp.exp(lr[:, at : at + 1]), shape)
            weight = jnp.broadcast_to(w[:, at : at + 1], shape)
            end = jnp.exp(-rate * (BLOCK - 1.0 - token))
            start = jnp.exp(-rate * token)
            decay = jnp.exp(-rate)
            parts[0].append(split(end))
            parts[1].append(split((BLOCK - 1.0 - token) * end))
            parts[2].append(jnp.where(first, 1.0, token + 1.0) * start)
            parts[3].append(decay * jnp.where(first, weight * start, end))
            for i, value in enumerate((end, start)):
                row = jnp.sum(weight * value, axis=0, keepdims=True)
                kk[i, at : at + 1, :] = jnp.where(first[:1], row, 0.0)
            if g == 0:
                rate_lanes, weight_lanes = rate, weight
            else:
                rate_lanes = jnp.where(own == g, rate, rate_lanes)
                weight_lanes = jnp.where(own == g, weight, weight_lanes)
        for i in range(3):
            lc[c, i] = jnp.concatenate(parts[i], 0).astype(BF16)
        turned = jnp.concatenate(parts[3], 0).T.astype(BF16)
        lrw[c, 0] = turned[:BLOCK]
        lrw[c, 1] = turned[BLOCK:]
        lanes = slice(c * LANES, (c + 1) * LANES)
        r_e[:, lanes] = rate_lanes
        w_e[:, lanes] = weight_lanes


def features_kernel(
    x, xh, gain, filt, lc, kk, r_e, nrm_out, q, k, v, p, inside, inv_out, s, f, inv, nrm
):
    channels = x.shape[1]
    step = pl.program_id(0)

    @pl.when(step == 0)
    def _():
        def add(i, carry):
            own, halo = carry
            lanes = pl.ds(pl.multiple_of(i * LANES, LANES), LANES)
            a = x[:, lanes].astype(F32)
            b = xh[:, lanes].astype(F32)
            return own + a * a, halo + b * b

        own, halo = lax.fori_loop(
            0,
            channels // LANES,
            add,
            (jnp.zeros((LANES, LANES), F32), jnp.zeros((8, LANES), F32)),
            unroll=4,
        )
        for rows, total in ((slice(0, 8), halo), (slice(8, 136), own)):
            mean = jnp.sum(total, axis=1, keepdims=True) * (1.0 / channels)
            inverse = lax.rsqrt(mean + EPSILON)
            inv[rows, :] = jnp.broadcast_to(inverse, total.shape)
        inv_out[...] = inv[...]

    for c in range(STEP):
        local = slice(c * LANES, (c + 1) * LANES)
        lanes = pl.ds(pl.multiple_of((step * STEP + c) * LANES, LANES), LANES)
        gains = gain[:, local]
        own = x[:, lanes].astype(F32) * inv[8:136, :]
        own = (own * gains).astype(BF16)
        nrm_out[c, 16:144, :] = own
        nrm[c, 8:136, :] = own.astype(F32)
        halo = xh[:, lanes].astype(F32) * inv[0:8, :]
        halo = (halo * gains).astype(BF16).astype(F32)
        nrm_out[c, 0:16, :] = jnp.concatenate([jnp.zeros_like(halo), halo], 0).astype(BF16)
        nrm[c, 0:8, :] = halo
        taps = [filt[j, 0:1, local] for j in range(21)]
        for r in range(0, LANES, 32):
            total = [jnp.zeros((32, LANES), F32) for _ in range(3)]
            for j in range(7):
                rows = nrm[c, 8 + r - j : 40 + r - j, :]
                for i in range(3):
                    total[i] = total[i] + taps[i * 7 + j] * rows
            q[c, r : r + 32, :] = total[0]
            k[c, r : r + 32, :] = total[1]
            v[c, r : r + 32, :] = total[2]
            product = total[1] * total[2]
            high = product.astype(BF16)
            p[0, c, r : r + 32, :] = high
            p[1, c, r : r + 32, :] = (product - high.astype(F32)).astype(BF16)
    for c in range(STEP):
        local = slice(c * LANES, (c + 1) * LANES)
        high, low = side_by_side(p[0, c]), side_by_side(p[1, c])
        table = lc[c].reshape(2 * LANES, LANES)
        sums = dot(
            jnp.concatenate([table, table], 1), jnp.concatenate([high, high, low, low], 0)
        )
        ends, ramps = own_group(sums[:LANES]), own_group(sums[LANES:])
        span = jnp.exp(-float(BLOCK) * r_e[:, local])
        s[:, local] = span * ends[:, :LANES] + ends[:, LANES:]
        f[0:32, local] = stacked(ends)
        f[32:64, local] = stacked(ramps)
        inside[c] = forward_blocks(p[0, c], kk[0, c * 8 : c * 8 + 8, :])


def forward_blocks(p, kernel):
    first = iota((BLOCK, LANES), 1) < BLOCK
    tiles = []
    for g in range(0, 8, 2):
        even, odd = (jnp.broadcast_to(kernel[i : i + 1], (BLOCK, LANES)) for i in (g, g + 1))
        even = pltpu.roll(even, BLOCK + 1, 1, stride=1, stride_axis=0)
        odd = pltpu.roll(odd, 1, 1, stride=1, stride_axis=0)
        tiles.append(jnp.where(first, even, odd).astype(BF16))
    return stacked(dot(jnp.concatenate(tiles, 1), by_group(side_by_side(p))))


def taken(grads, c, streams, taps, first, rows):
    total = None
    for i, stream in enumerate(streams):
        for j in range(7):
            term = taps[stream * 7 + j] * grads[c, i, first + j : first + j + rows, :]
            total = term if total is None else total + term
    return total


def tap_gradients(grads, nrm, c, count):
    sums = [jnp.zeros((8, LANES), F32) for _ in range(7 * count)]
    for r in range(0, LANES, 32):
        items = [grads[c, i, 8 + r : 40 + r, :] for i in range(count)]
        for j in range(7):
            rows = nrm[c, 16 + r - j : 48 + r - j, :]
            for i in range(count):
                term = (items[i] * rows).reshape(4, 8, LANES)
                sums[i * 7 + j] = sums[i * 7 + j] + jnp.sum(term, axis=0)
    return [jnp.sum(item, axis=0, keepdims=True) for item in sums]


def clear_ends(grads, count):
    @pl.when(pl.program_id(0) == 0)
    def _():
        for i in range(count):
            grads[:, i, 0:8, :] = jnp.zeros((STEP, 8, LANES), F32)
            grads[:, i, 136:144, :] = jnp.zeros((STEP, 8, LANES), F32)


def output_kernel(
    inside, lrw, e, f, r_e, q, p, x, skip, g0, g1, g2, nrm_in, filt, out, gn, fg, grads, nrm
):
    clear_ends(grads, 1)
    for c in range(STEP):
        nrm[c] = nrm_in[c].astype(F32)
        local = slice(c * LANES, (c + 1) * LANES)
        state = e[:, local]
        second = f[:, local] + jnp.exp(-float(BLOCK) * r_e[:, local]) * state
        states = jnp.concatenate([state, second], 1).astype(BF16)
        carried = stacked(dot(lrw[c, 0], by_group(states)))
        product = p[0, c].astype(F32) + p[1, c].astype(F32)
        modal = inside[c] + carried + skip[:, local] * product
        query = q[c]
        arrived = joined((g0, g1, g2), local)
        out[:, local] = (x[:, local].astype(F32) + query * modal).astype(BF16)
        grads[c, 0, 8:136, :] = arrived * modal
        skip_grad = jnp.sum(arrived * query * product, axis=0, keepdims=True)
        taps = [filt[j, 0:1, local] for j in range(7)]
        gn[c, 0:8, :] = taken(grads, c, (0,), taps, 0, 8)
        for r in range(8, 136, 32):
            gn[c, r : r + 32, :] = taken(grads, c, (0,), taps, r, 32)
        fg[:, local] = jnp.concatenate(tap_gradients(grads, nrm, c, 1) + [skip_grad], 0)


def adjoint_kernel(g0, g1, g2, q, lc, w_e, r_e, gm, a, b):
    for c in range(STEP):
        local = slice(c * LANES, (c + 1) * LANES)
        grad = (joined((g0, g1, g2), local) * q[c]).astype(BF16)
        gm[c] = grad
        sides = side_by_side(grad)
        none = jnp.zeros_like(sides)
        sides = jnp.concatenate(
            [jnp.concatenate([sides, none], 1), jnp.concatenate([none, sides], 1)], 0
        )
        sums = own_group(dot(lc[c, 0], sides))
        starts, ramps = sums[:, : 2 * LANES], sums[:, 2 * LANES :]
        span = jnp.exp(-float(BLOCK) * r_e[:, local])
        first = w_e[:, local] * (starts[:, :LANES] + span * starts[:, LANES:])
        a[:, local] = first.astype(BF16)
        b[0:32, local] = stacked(starts)
        b[32:64, local] = stacked(ramps)


def backward_kernel(p, gm, kk, back, by_lag):
    first = iota((BLOCK, LANES), 1) < BLOCK
    both = iota((LANES, LANES), 0) + iota((LANES, LANES), 1)
    same = iota((LANES, LANES), 0) // BLOCK == iota((LANES, LANES), 1) // BLOCK
    flip = (same & (both % BLOCK == BLOCK - 1)).astype(BF16)
    for c in range(STEP):
        grads = by_group(side_by_side(gm[c]))
        tiles = []
        for g in range(0, 8, 2):
            even, odd = (
                jnp.broadcast_to(kk[0, c * 8 + i : c * 8 + i + 1, :], (BLOCK, LANES))
                for i in (g, g + 1)
            )
            even = pltpu.roll(even, 0, 1, stride=1, stride_axis=0)
            odd = pltpu.roll(odd, BLOCK, 1, stride=1, stride_axis=0)
            tiles.append(jnp.where(first, even, odd).astype(BF16))
        back[c] = stacked(dot(jnp.concatenate(tiles, 1), grads))
        sides = jnp.concatenate([side_by_side(p[0, c]), side_by_side(p[1, c])], 0)
        sides = dot(flip, sides).astype(BF16)
        crossed = lax.dot_general(
            sides, grads, (((1,), (1,)), ((), ())), preferred_element_type=F32
        )
        crossed = crossed[:BLOCK] + crossed[BLOCK:]
        for g in range(8):
            tile = crossed[:, g // 2 * LANES : (g // 2 + 1) * LANES]
            tile = jnp.where(first if g % 2 == 0 else ~first, tile, 0.0)
            tile = pltpu.roll(tile, g % 2 * BLOCK, 1, stride=1, stride_axis=0)
            by_lag[c * 8 + g : c * 8 + g + 1, :] = jnp.sum(tile, axis=0, keepdims=True)


def mixer_kernel(
    back, lrw, a, b, w_e, r_e, gm, k, v, gn0, nrm_in, filt, skip, gain, x, inv,
    gn, fg, hx, part, grads, nrm,
):
    clear_ends(grads, 2)

    @pl.when(pl.program_id(0) == 0)
    def _():
        hx[...] = jnp.zeros_like(hx)

    for c in range(STEP):
        nrm[c] = nrm_in[c].astype(F32)
        local = slice(c * LANES, (c + 1) * LANES)
        second = a[:, local].astype(F32)
        span = jnp.exp(-float(BLOCK) * r_e[:, local])
        first = w_e[:, local] * b[:, local] + span * second
        states = jnp.concatenate([first, second], 1).astype(BF16)
        carried = stacked(dot(lrw[c, 0], by_group(states)))
        modal = gm[c].astype(F32)
        product = back[c] + carried + skip[:, local] * modal
        grads[c, 0, 8:136, :] = product * v[c]
        grads[c, 1, 8:136, :] = product * k[c]
        gains = gain[:, local]
        taps = [filt[j, 0:1, local] for j in range(21)]
        part[:, local] = (gn0[c, 0:8, :] + taken(grads, c, (1, 2), taps, 0, 8)).astype(BF16)
        gain_grad = jnp.zeros((8, LANES), F32)
        for r in range(0, LANES, 32):
            total = gn0[c, 8 + r : 40 + r, :] + taken(grads, c, (1, 2), taps, 8 + r, 32)
            gn[c, r : r + 32, :] = total
            xhat = x[r : r + 32, local].astype(F32) * inv[8 + r : 40 + r, :]
            both = total * xhat
            gain_grad = gain_grad + jnp.sum(both.reshape(4, 8, LANES), axis=0)
            hx[r : r + 32, :] += both * gains
        gain_grad = jnp.sum(gain_grad, axis=0, keepdims=True)
        rows = tap_gradients(grads, nrm, c, 2) + [gain_grad, jnp.zeros((1, LANES), F32)]
        fg[:, local] = jnp.concatenate(rows, 0)


def final_kernel(
    gn, g0, g1, g2, fg0, fg, hx, part, x, x_last, inv, gain, gain_all, out, cg, mean
):
    channels = x_last.shape[1]
    step = pl.program_id(0)

    @pl.when(step == 0)
    def _():
        def add(i, total):
            lanes = pl.ds(pl.multiple_of(i * LANES, LANES), LANES)
            xhat = x_last[8:16, lanes].astype(F32) * inv[128:136, :]
            return total + part[:, lanes].astype(F32) * gain_all[:, lanes] * xhat

        extra = lax.fori_loop(
            0, channels // LANES, add, jnp.zeros((8, LANES), F32), unroll=4
        )
        total = jnp.concatenate([hx[:120], hx[120:] + extra], 0)
        total = jnp.sum(total, axis=1, keepdims=True) * (1.0 / channels)
        mean[...] = jnp.broadcast_to(total, mean.shape)

    for c in range(STEP):
        local = slice(c * LANES, (c + 1) * LANES)
        lanes = pl.ds(pl.multiple_of((step * STEP + c) * LANES, LANES), LANES)
        arrived = joined((g0, g1, g2), local)
        extra = part[:, lanes].astype(F32)
        own = gn[c]
        own = jnp.concatenate([own[:120], own[120:] + extra], 0)
        xhat = x[:, local].astype(F32) * inv[8:136, :]
        result = arrived + inv[8:136, :] * (own * gain[:, local] - xhat * mean[...])
        out[:, local] = result.astype(BF16)
        fixed = jnp.sum(extra * xhat[120:], axis=0, keepdims=True)
        sources = [fg0[i : i + 1, local] for i in range(7)]
        sources += [fg[i : i + 1, local] for i in range(14)]
        sources += [fg[14:15, local] + fixed, fg0[7:8, local]]
        for i, source in enumerate(sources):
            cg[i, 0:1, local] = source


def modes_kernel(a, b, e, f, r_e, w_e, by_lag, lr, w, residue_out, rate_out):
    groups = lr.shape[1]
    chunks = e.shape[1] // LANES

    def chunk(i, total):
        lanes = pl.ds(pl.multiple_of(i * LANES, LANES), LANES)
        rate = r_e[:, lanes]
        weight = w_e[:, lanes]
        span = jnp.exp(-float(BLOCK) * rate)
        state0 = e[:, lanes]
        state1 = f[0:16, lanes] + span * state0
        adjoint1 = a[:, lanes].astype(F32)
        adjoint0 = weight * b[16:32, lanes] + span * adjoint1
        one = (state0 * b[0:16, lanes] + state1 * b[16:32, lanes]) * jnp.exp(-rate)
        two = weight * (state0 * b[32:48, lanes] + state1 * b[48:64, lanes])
        two = two + adjoint0 * f[32:48, lanes] + adjoint1 * f[48:64, lanes]
        two = two + BLOCK * span * (adjoint0 * state0 + adjoint1 * state1)
        both = jnp.concatenate([one, two], 0)
        high = both.astype(BF16)
        low = (both - high.astype(F32)).astype(BF16)
        shape = (LANES, groups)
        hot = (iota(shape, 1) == i * 8 + iota(shape, 0) // 16).astype(BF16)
        return total + dot(jnp.concatenate([high, low], 0), hot)

    totals = lax.fori_loop(0, chunks, chunk, jnp.zeros((64, groups), F32), unroll=8)
    totals = totals[:32] + totals[32:]
    lag = (iota((LANES, groups), 0) - (BLOCK - 1)).astype(F32)
    lags = jnp.where(lag >= 0.0, by_lag[...].T, 0.0)
    lag = jnp.maximum(lag, 0.0)
    for m in range(16):
        rate = jnp.exp(lr[m : m + 1, :])
        terms = jnp.exp(-rate * lag) * lags
        first = jnp.sum(terms, axis=0, keepdims=True)
        second = jnp.sum(terms * lag, axis=0, keepdims=True) * jnp.exp(rate)
        residue_out[m : m + 1, :] = first + totals[m : m + 1, :]
        decay = w[m : m + 1, :] * second + totals[16 + m : 17 + m, :]
        rate_out[m : m + 1, :] = decay * (-jnp.exp(-rate) * rate)


def levels_of(count):
    levels = []
    stride = 1
    while stride < count:
        size = 2 if stride == 1 else min(4, count // stride)
        levels.append((stride, size))
        stride *= size
    return levels


def after(value, *others):
    return lax.optimization_barrier((value, *others))[0]


def shard_numbers(rows):
    count = lax.axis_size("seq")
    shard = lax.axis_index("seq")
    found = {"even": shard % 2 == 0}
    for reverse in (False, True):
        low = 0
        for number, (stride, size) in enumerate(levels_of(count)):
            digit = (shard // stride) % size
            place = size - 1 - digit if reverse else digit
            found[reverse, number, "own"] = (rows * stride * (size - 1 - place)).astype(F32)
            if number > 1:
                found[reverse, number, "low"] = (rows * low).astype(F32)
            found[reverse, number, "place"] = (rows * stride * place).astype(F32)
            for h in range(1, size):
                found[reverse, number, "earlier", h] = jnp.where(h <= place, 1.0, 0.0)
                away = rows * stride * ((h - 1 - place) % size)
                found[reverse, number, "away", h] = away.astype(F32)
            if number:
                low = low + place * stride
    return found


class Prefix:
    def __init__(self, local, rate, rows, reverse, column):
        self.count = lax.axis_size("seq")
        self.local, self.rate, self.rows, self.reverse = local, rate, rows, reverse
        self.column = column
        self.value = local
        self.levels = levels_of(self.count)
        self.above = 0.0

    def get(self, *name):
        return self.column((self.reverse,) + name)

    def mine(self, value):
        half = value.shape[1] // 2
        return jnp.where(self.column("even"), value[:, :half], value[:, half:])

    def send(self, number):
        stride, size = self.levels[number]
        last = stride * size == self.count
        sign = -1 if self.reverse else 1
        self.got = []
        for h in range(1, size):
            pairs = []
            for i in range(self.count):
                there = (i // stride) % size + sign * h
                if last and not 0 <= there < size:
                    continue
                pairs.append((i, i + (there % size - (i // stride) % size) * stride))
            self.got.append(lax.ppermute(self.value, "seq", pairs))

    def join(self, number, *others):
        stride, size = self.levels[number]
        last = stride * size == self.count
        rate = self.rate if number == 0 else self.mine(self.rate)
        span = float(self.rows * stride)
        got = self.got
        if others:
            got = [after(item, *others) for item in got]
        own = self.value.astype(F32)
        group = own * jnp.exp(-rate * self.get(number, "own"))
        before = jnp.zeros_like(own)
        for h in range(1, size):
            item = got[h - 1].astype(F32)
            earlier = self.get(number, "earlier", h)
            before = before + item * (earlier * jnp.exp(-rate * (span * (h - 1))))
            if not last:
                group = group + item * jnp.exp(-rate * self.get(number, "away", h))
        if number == 0:
            self.near = before
            group = self.mine(group)
        else:
            if number > 1:
                before = before * jnp.exp(-rate * self.get(number, "low"))
            self.above = self.above + before
        self.value = group.astype(self.local.dtype)

    def swap(self):
        mine = self.above.astype(self.local.dtype)
        other = lax.ppermute(mine, "seq", [(i, i ^ 1) for i in range(self.count)])
        even = self.column("even")
        low = jnp.where(even, mine, other)
        high = jnp.where(even, other, mine)
        above = jnp.concatenate([low, high], 1).astype(F32)
        result = self.near + above * jnp.exp(-self.rate * self.get(0, "place"))
        return result.astype(self.local.dtype)


def on_device(section_input, sent_grad, norm_gain, short_filter, log_rate, residue, skip_gain):
    x = section_input[0]
    rows, channels = x.shape
    groups = log_rate.shape[2]
    chunks = channels // LANES
    sections = lax.axis_size("section")
    count = lax.axis_size("seq")
    filt, gain, skip = short_filter.reshape(-1, 1, channels), norm_gain, skip_gain
    names, numbers = zip(*shard_numbers(rows).items())
    lr, w, *numbers = lax.optimization_barrier((log_rate[0], residue[0], *numbers))
    column = dict(zip(names, numbers)).__getitem__

    ring = [(i, (i - 1) % sections) for i in range(sections)]
    cuts = (0, rows * 3 // 8, rows * 7 // 8, rows)
    g = [
        lax.ppermute(sent_grad[0, low:high], "section", ring)
        for low, high in zip(cuts[:-1], cuts[1:])
    ]
    arrived = [(item, (item.shape[0], WIDE), lambda i: (0, i)) for item in g]
    halo = lax.ppermute(x[rows - 8 :], "seq", [(i, i + 1) for i in range(count - 1)])

    full = lambda i: (0, 0)
    lane = lambda i: (0, i)
    block = lambda i: (i, 0, 0)
    cube = (STEP, LANES, LANES)
    tall = (STEP, LANES + 8, LANES)
    normal = (STEP, LANES + 16, LANES)
    grid = (chunks // STEP,)
    table_step = min(TABLE_STEP, chunks)
    table_groups = 8 * table_step
    lc, lrw, kk, r_e, w_e = call(
        table_kernel,
        (chunks // table_step,),
        [(lr, (16, table_groups), lane), (w, (16, table_groups), lane)],
        [
            (
                (chunks, 3, LANES, LANES),
                BF16,
                (table_step, 3, LANES, LANES),
                lambda i: (i, 0, 0, 0),
            ),
            (
                (chunks, 2, BLOCK, LANES),
                BF16,
                (table_step, 2, BLOCK, LANES),
                lambda i: (i, 0, 0, 0),
            ),
            ((2, groups, LANES), F32, (2, table_groups, LANES), lambda i: (0, i, 0)),
            ((16, channels), F32, (16, table_step * LANES), lane),
            ((16, channels), F32, (16, table_step * LANES), lane),
        ],
        micros=0,
        name="tables",
    )
    wide16 = (16, WIDE)
    nrm, q, k, v, p, inside, inv, s, f = call(
        features_kernel,
        grid,
        [
            (x, (rows, channels), full),
            (after(halo, g[0]), (8, channels), full),
            (gain, (1, WIDE), lane),
            (filt, (21, 1, WIDE), lambda i: (0, 0, i)),
            (lc, (STEP, 2, LANES, LANES), lambda i: (i, 0, 0, 0)),
            (kk, (1, 8 * STEP, LANES), lambda i: (0, i, 0)),
            (r_e, wide16, lane),
        ],
        [
            ((chunks, LANES + 16, LANES), BF16, normal, block),
            ((chunks, LANES, LANES), F32, cube, block),
            ((chunks, LANES, LANES), F32, cube, block),
            ((chunks, LANES, LANES), F32, cube, block),
            ((2, chunks, LANES, LANES), BF16, (2,) + cube, lambda i: (0, i, 0, 0)),
            ((chunks, LANES, LANES), F32, cube, block),
            ((LANES + 8, LANES), F32, (LANES + 8, LANES), full),
            ((16, channels), F32, wide16, lane),
            ((64, channels), F32, (64, WIDE), lane),
        ],
        scratch=[pltpu.VMEM((LANES + 8, LANES), F32), pltpu.VMEM(tall, F32)],
        micros=0,
        name="features",
    )
    ahead = Prefix(after(s, g[1]), r_e, rows, False, column)
    ahead.send(0)
    ahead.join(0)
    ahead.send(1)
    q_late = after(q, ahead.value)
    gm, a_local, b = call(
        adjoint_kernel,
        grid,
        [
            *arrived,
            (q_late, cube, block),
            (lc, (STEP, 1, LANES, LANES), lambda i: (i, 2, 0, 0)),
            (w_e, wide16, lane),
            (r_e, wide16, lane),
        ],
        [
            ((chunks, LANES, LANES), BF16, cube, block),
            ((16, channels), BF16, wide16, lane),
            ((64, channels), F32, (64, WIDE), lane),
        ],
        micros=0,
        name="adjoint",
    )
    behind = Prefix(after(a_local, *ahead.got), r_e, rows, True, column)
    behind.send(0)
    ahead.join(1, a_local)
    ahead.send(2)
    behind.join(0)
    behind.send(1)
    gm_late = after(gm, behind.value, ahead.value)
    back, by_lag = call(
        backward_kernel,
        grid,
        [
            (p, (2,) + cube, lambda i: (0, i, 0, 0)),
            (gm_late, cube, block),
            (kk, (1, 8 * STEP, LANES), lambda i: (1, i, 0)),
        ],
        [
            ((chunks, LANES, LANES), F32, cube, block),
            ((groups, LANES), F32, (8 * STEP, LANES), lambda i: (i, 0)),
        ],
        micros=6,
        name="backward",
    )
    behind.join(1, by_lag)
    behind.send(2)
    ahead.join(2, by_lag)
    e = after(ahead.swap(), behind.value)
    block_out, gn0, fg0 = call(
        output_kernel,
        grid,
        [
            (inside, cube, block),
            (lrw, (STEP, 1, BLOCK, LANES), lambda i: (i, 0, 0, 0)),
            (e, wide16, lane),
            (f, wide16, lane),
            (r_e, wide16, lane),
            (q, cube, block),
            (p, (2,) + cube, lambda i: (0, i, 0, 0)),
            (x, (rows, WIDE), lane),
            (skip, (1, WIDE), lane),
            *arrived,
            (nrm, normal, block),
            (filt, (21, 1, WIDE), lambda i: (0, 0, i)),
        ],
        [
            ((rows, channels), BF16, (rows, WIDE), lane),
            ((chunks, LANES + 8, LANES), F32, tall, block),
            ((8, channels), F32, (8, WIDE), lane),
        ],
        scratch=[pltpu.VMEM((STEP, 1, LANES + 16, LANES), F32), pltpu.VMEM(normal, F32)],
        micros=8,
        name="output",
    )
    behind.join(2, fg0)
    a = behind.swap()
    gn, fg, hx, part = call(
        mixer_kernel,
        grid,
        [
            (back, cube, block),
            (lrw, (STEP, 1, BLOCK, LANES), lambda i: (i, 1, 0, 0)),
            (a, wide16, lane),
            (b, wide16, lambda i: (1, i)),
            (w_e, wide16, lane),
            (r_e, wide16, lane),
            (gm, cube, block),
            (k, cube, block),
            (v, cube, block),
            (gn0, tall, block),
            (nrm, normal, block),
            (filt, (21, 1, WIDE), lambda i: (0, 0, i)),
            (skip, (1, WIDE), lane),
            (gain, (1, WIDE), lane),
            (x, (rows, WIDE), lane),
            (inv, (LANES + 8, LANES), full),
        ],
        [
            ((chunks, LANES, LANES), F32, cube, block),
            ((16, channels), F32, wide16, lane),
            ((LANES, LANES), F32, (LANES, LANES), full),
            ((8, channels), BF16, (8, WIDE), lane),
        ],
        scratch=[pltpu.VMEM((STEP, 2, LANES + 16, LANES), F32), pltpu.VMEM(normal, F32)],
        micros=10,
        name="mixer",
    )
    part = lax.ppermute(part, "seq", [(i + 1, i) for i in range(count - 1)])
    whole = lambda value: (value, value.shape, lambda i: (0,) * value.ndim)
    residue_grads, rate_grads = call(
        modes_kernel,
        (1,),
        [whole(value) for value in (a, b, e, f, r_e, w_e, by_lag, lr, w)],
        [((16, groups), F32, (16, groups), full)] * 2,
        micros=3,
        name="modes",
    )
    input_grad, channel_grads = call(
        final_kernel,
        grid,
        [
            (gn, cube, block),
            *arrived,
            (fg0, (8, WIDE), lane),
            (fg, wide16, lane),
            (hx, (LANES, LANES), full),
            (part, (8, channels), full),
            (x, (rows, WIDE), lane),
            (x, (16, channels), lambda i: (rows // 16 - 1, 0)),
            (inv, (LANES + 8, LANES), full),
            (gain, (1, WIDE), lane),
            (gain, (1, channels), full),
        ],
        [
            ((rows, channels), BF16, (rows, WIDE), lane),
            ((23, 1, channels), F32, (23, 1, WIDE), lambda i: (0, 0, i)),
        ],
        scratch=[pltpu.VMEM((LANES, LANES), F32)],
        micros=4,
        name="final",
    )
    return (
        block_out[None],
        input_grad[None],
        channel_grads.reshape(1, 1, 23, channels),
        residue_grads[None, None],
        rate_grads[None, None],
    )


def solution(mesh):
    placed = (
        P("section", "seq", None),
        P("section", "seq", None),
        P("section", None),
        P("section", None, None),
        P("section", None, None),
        P("section", None, None),
        P("section", None),
    )
    return jax.shard_map(
        on_device,
        mesh=mesh,
        in_specs=placed,
        out_specs=(
            P("section", "seq", None),
            P("section", "seq", None),
            P("section", "seq", None, None),
            P("section", "seq", None, None),
            P("section", "seq", None, None),
        ),
        check_vma=False,
    )
```

```python
import jax
import jax.numpy as jnp
from jax import lax
from jax.experimental import pallas as pl
from jax.experimental.pallas import tpu as pltpu
from jax.sharding import PartitionSpec as P

EPSILON = 1e-06
F32 = jnp.float32
BF16 = jnp.bfloat16
LANES = 128
STEP = 8
WIDE = STEP * LANES
BLOCK = 64
TABLE_STEP = 16
VMEM_LIMIT = 20 * 1024 * 1024


def iota(shape, axis):
    return lax.broadcasted_iota(jnp.int32, shape, axis)


def dot(a, b):
    return jnp.dot(a, b, preferred_element_type=F32)


def call(kernel, grid, ins, outs, scratch=(), micros=1.0, name=None):
    total = sum(a.size * a.dtype.itemsize for a, _, _ in ins)
    for shape, dtype, _, _ in outs:
        size = jnp.dtype(dtype).itemsize
        for n in shape:
            size *= n
        total += size
    return pl.pallas_call(
        kernel,
        grid=grid,
        in_specs=[pl.BlockSpec(b, m) for _, b, m in ins],
        out_specs=[pl.BlockSpec(b, m) for _, _, b, m in outs],
        out_shape=[jax.ShapeDtypeStruct(s, d) for s, d, _, _ in outs],
        scratch_shapes=list(scratch),
        compiler_params=pltpu.CompilerParams(
            dimension_semantics=("arbitrary",) * len(grid), vmem_limit_bytes=VMEM_LIMIT
        ),
        cost_estimate=pl.CostEstimate(
            flops=int(micros * 1.0e9),
            bytes_accessed=int(total) if micros else 0,
            transcendentals=0,
        ),
        name=name,
    )(*[a for a, _, _ in ins])


def lane_group(shape):
    return (iota(shape, 1) % LANES) // 16


def by_group(rows):
    own = lane_group(rows.shape)
    zero = jnp.zeros_like(rows)
    return jnp.concatenate([jnp.where(own == g, rows, zero) for g in range(8)], 0)


def own_group(rows):
    own = lane_group((16, rows.shape[1]))
    kept = rows[:16]
    for g in range(1, 8):
        kept = jnp.where(own == g, rows[16 * g : 16 * g + 16], kept)
    return kept


def side_by_side(rows):
    return jnp.concatenate([rows[:BLOCK], rows[BLOCK:]], 1)


def joined(parts, lanes):
    return jnp.concatenate([part[:, lanes] for part in parts], 0).astype(F32)


def stacked(rows):
    return jnp.concatenate([rows[:, :LANES], rows[:, LANES:]], 0)


def table_kernel(lr, w, lc, lrw, kk, r_e, w_e):
    shape = (16, LANES)
    first = iota(shape, 1) < BLOCK
    token = (iota(shape, 1) % BLOCK).astype(F32)
    own = lane_group(shape)

    def split(value):
        high = value.astype(BF16).astype(F32)
        return jnp.where(first, high, value - high)

    for c in range(lc.shape[0]):
        parts = [[] for _ in range(4)]
        rate_lanes = weight_lanes = None
        for g in range(8):
            at = c * 8 + g
            rate = jnp.broadcast_to(jnp.exp(lr[:, at : at + 1]), shape)
            weight = jnp.broadcast_to(w[:, at : at + 1], shape)
            end = jnp.exp(-rate * (BLOCK - 1.0 - token))
            start = jnp.exp(-rate * token)
            decay = jnp.exp(-rate)
            parts[0].append(split(end))
            parts[1].append(split((BLOCK - 1.0 - token) * end))
            parts[2].append(jnp.where(first, 1.0, token + 1.0) * start)
            parts[3].append(decay * jnp.where(first, weight * start, end))
            for i, value in enumerate((end, start)):
                row = jnp.sum(weight * value, axis=0, keepdims=True)
                kk[i, at : at + 1, :] = jnp.where(first[:1], row, 0.0)
            if g == 0:
                rate_lanes, weight_lanes = rate, weight
            else:
                rate_lanes = jnp.where(own == g, rate, rate_lanes)
                weight_lanes = jnp.where(own == g, weight, weight_lanes)
        for i in range(3):
            lc[c, i] = jnp.concatenate(parts[i], 0).astype(BF16)
        turned = jnp.concatenate(parts[3], 0).T.astype(BF16)
        lrw[c, 0] = turned[:BLOCK]
        lrw[c, 1] = turned[BLOCK:]
        lanes = slice(c * LANES, (c + 1) * LANES)
        r_e[:, lanes] = rate_lanes
        w_e[:, lanes] = weight_lanes


def features_kernel(
    x, xh, gain, filt, lc, kk, r_e, nrm_out, q, k, v, p, inside, inv_out, s, f, inv, nrm
):
    channels = x.shape[1]
    step = pl.program_id(0)

    @pl.when(step == 0)
    def _():
        def add(i, carry):
            own, halo = carry
            lanes = pl.ds(pl.multiple_of(i * LANES, LANES), LANES)
            a = x[:, lanes].astype(F32)
            b = xh[:, lanes].astype(F32)
            return own + a * a, halo + b * b

        own, halo = lax.fori_loop(
            0,
            channels // LANES,
            add,
            (jnp.zeros((LANES, LANES), F32), jnp.zeros((8, LANES), F32)),
            unroll=4,
        )
        for rows, total in ((slice(0, 8), halo), (slice(8, 136), own)):
            mean = jnp.sum(total, axis=1, keepdims=True) * (1.0 / channels)
            inverse = lax.rsqrt(mean + EPSILON)
            inv[rows, :] = jnp.broadcast_to(inverse, total.shape)
        inv_out[...] = inv[...]

    for c in range(STEP):
        local = slice(c * LANES, (c + 1) * LANES)
        lanes = pl.ds(pl.multiple_of((step * STEP + c) * LANES, LANES), LANES)
        gains = gain[:, local]
        own = x[:, lanes].astype(F32) * inv[8:136, :]
        own = (own * gains).astype(BF16)
        nrm_out[c, 16:144, :] = own
        nrm[c, 8:136, :] = own.astype(F32)
        halo = xh[:, lanes].astype(F32) * inv[0:8, :]
        halo = (halo * gains).astype(BF16).astype(F32)
        nrm_out[c, 0:16, :] = jnp.concatenate([jnp.zeros_like(halo), halo], 0).astype(BF16)
        nrm[c, 0:8, :] = halo
        taps = [filt[j, 0:1, local] for j in range(21)]
        for r in range(0, LANES, 32):
            total = [jnp.zeros((32, LANES), F32) for _ in range(3)]
            for j in range(7):
                rows = nrm[c, 8 + r - j : 40 + r - j, :]
                for i in range(3):
                    total[i] = total[i] + taps[i * 7 + j] * rows
            q[c, r : r + 32, :] = total[0]
            k[c, r : r + 32, :] = total[1]
            v[c, r : r + 32, :] = total[2]
            product = total[1] * total[2]
            high = product.astype(BF16)
            p[0, c, r : r + 32, :] = high
            p[1, c, r : r + 32, :] = (product - high.astype(F32)).astype(BF16)
    for c in range(STEP):
        local = slice(c * LANES, (c + 1) * LANES)
        high, low = side_by_side(p[0, c]), side_by_side(p[1, c])
        table = lc[c].reshape(2 * LANES, LANES)
        sums = dot(
            jnp.concatenate([table, table], 1), jnp.concatenate([high, high, low, low], 0)
        )
        ends, ramps = own_group(sums[:LANES]), own_group(sums[LANES:])
        span = jnp.exp(-float(BLOCK) * r_e[:, local])
        s[:, local] = span * ends[:, :LANES] + ends[:, LANES:]
        f[0:32, local] = stacked(ends)
        f[32:64, local] = stacked(ramps)
        inside[c] = forward_blocks(p[0, c], kk[0, c * 8 : c * 8 + 8, :])


def forward_blocks(p, kernel):
    first = iota((BLOCK, LANES), 1) < BLOCK
    tiles = []
    for g in range(0, 8, 2):
        even, odd = (jnp.broadcast_to(kernel[i : i + 1], (BLOCK, LANES)) for i in (g, g + 1))
        even = pltpu.roll(even, BLOCK + 1, 1, stride=1, stride_axis=0)
        odd = pltpu.roll(odd, 1, 1, stride=1, stride_axis=0)
        tiles.append(jnp.where(first, even, odd).astype(BF16))
    return stacked(dot(jnp.concatenate(tiles, 1), by_group(side_by_side(p))))


def taken(grads, c, streams, taps, first, rows):
    total = None
    for i, stream in enumerate(streams):
        for j in range(7):
            term = taps[stream * 7 + j] * grads[c, i, first + j : first + j + rows, :]
            total = term if total is None else total + term
    return total


def tap_gradients(grads, nrm, c, count):
    sums = [jnp.zeros((8, LANES), F32) for _ in range(7 * count)]
    for r in range(0, LANES, 32):
        items = [grads[c, i, 8 + r : 40 + r, :] for i in range(count)]
        for j in range(7):
            rows = nrm[c, 16 + r - j : 48 + r - j, :]
            for i in range(count):
                term = (items[i] * rows).reshape(4, 8, LANES)
                sums[i * 7 + j] = sums[i * 7 + j] + jnp.sum(term, axis=0)
    return [jnp.sum(item, axis=0, keepdims=True) for item in sums]


def clear_ends(grads, count):
    @pl.when(pl.program_id(0) == 0)
    def _():
        for i in range(count):
            grads[:, i, 0:8, :] = jnp.zeros((STEP, 8, LANES), F32)
            grads[:, i, 136:144, :] = jnp.zeros((STEP, 8, LANES), F32)


def output_kernel(
    inside, lrw, e, f, r_e, q, p, x, skip, g0, g1, g2, nrm_in, filt, out, gn, fg, grads, nrm
):
    clear_ends(grads, 1)
    for c in range(STEP):
        nrm[c] = nrm_in[c].astype(F32)
        local = slice(c * LANES, (c + 1) * LANES)
        state = e[:, local]
        second = f[:, local] + jnp.exp(-float(BLOCK) * r_e[:, local]) * state
        states = jnp.concatenate([state, second], 1).astype(BF16)
        carried = stacked(dot(lrw[c, 0], by_group(states)))
        product = p[0, c].astype(F32) + p[1, c].astype(F32)
        modal = inside[c] + carried + skip[:, local] * product
        query = q[c]
        arrived = joined((g0, g1, g2), local)
        out[:, local] = (x[:, local].astype(F32) + query * modal).astype(BF16)
        grads[c, 0, 8:136, :] = arrived * modal
        skip_grad = jnp.sum(arrived * query * product, axis=0, keepdims=True)
        taps = [filt[j, 0:1, local] for j in range(7)]
        gn[c, 0:8, :] = taken(grads, c, (0,), taps, 0, 8)
        for r in range(8, 136, 32):
            gn[c, r : r + 32, :] = taken(grads, c, (0,), taps, r, 32)
        fg[:, local] = jnp.concatenate(tap_gradients(grads, nrm, c, 1) + [skip_grad], 0)


def adjoint_kernel(g0, g1, g2, q, lc, w_e, r_e, gm, a, b):
    for c in range(STEP):
        local = slice(c * LANES, (c + 1) * LANES)
        grad = (joined((g0, g1, g2), local) * q[c]).astype(BF16)
        gm[c] = grad
        sides = side_by_side(grad)
        none = jnp.zeros_like(sides)
        sides = jnp.concatenate(
            [jnp.concatenate([sides, none], 1), jnp.concatenate([none, sides], 1)], 0
        )
        sums = own_group(dot(lc[c, 0], sides))
        starts, ramps = sums[:, : 2 * LANES], sums[:, 2 * LANES :]
        span = jnp.exp(-float(BLOCK) * r_e[:, local])
        first = w_e[:, local] * (starts[:, :LANES] + span * starts[:, LANES:])
        a[:, local] = first.astype(BF16)
        b[0:32, local] = stacked(starts)
        b[32:64, local] = stacked(ramps)


def lags_kernel(p, gm, by_lag):
    first = iota((1, LANES), 1) < BLOCK
    shape = (BLOCK, LANES)
    causal = iota(shape, 1) % BLOCK + iota(shape, 0) >= BLOCK - 1
    both = iota((LANES, LANES), 0) + iota((LANES, LANES), 1)
    same = iota((LANES, LANES), 0) // BLOCK == iota((LANES, LANES), 1) // BLOCK
    flip = (same & (both % BLOCK == BLOCK - 1)).astype(BF16)
    for c in range(STEP):
        grads = by_group(side_by_side(gm[c]))
        sides = jnp.concatenate([side_by_side(p[0, c]), side_by_side(p[1, c])], 0)
        sides = dot(flip, sides).astype(BF16)
        crossed = lax.dot_general(
            sides, grads, (((1,), (1,)), ((), ())), preferred_element_type=F32
        )
        crossed = crossed[:BLOCK] + crossed[BLOCK:]
        for g in range(0, 8, 2):
            tile = jnp.where(causal, crossed[:, g * BLOCK : (g + 2) * BLOCK], 0.0)
            tile = pltpu.roll(tile, BLOCK + 1, 1, stride=1, stride_axis=0)
            tile = jnp.sum(tile, axis=0, keepdims=True)
            at = c * 8 + g
            by_lag[at : at + 1, :] = jnp.where(first, tile, 0.0)
            by_lag[at + 1 : at + 2, :] = jnp.where(first, pltpu.roll(tile, BLOCK, 1), 0.0)


def backward_kernel(gm, kk, back):
    first = iota((BLOCK, LANES), 1) < BLOCK
    for c in range(STEP):
        tiles = []
        for g in range(0, 8, 2):
            even, odd = (
                jnp.broadcast_to(kk[0, c * 8 + i : c * 8 + i + 1, :], (BLOCK, LANES))
                for i in (g, g + 1)
            )
            even = pltpu.roll(even, 0, 1, stride=1, stride_axis=0)
            odd = pltpu.roll(odd, BLOCK, 1, stride=1, stride_axis=0)
            tiles.append(jnp.where(first, even, odd).astype(BF16))
        back[c] = stacked(dot(jnp.concatenate(tiles, 1), by_group(side_by_side(gm[c]))))


def mixer_kernel(
    back, lrw, a, b, w_e, r_e, gm, k, v, gn0, nrm_in, filt, skip, gain, x, inv,
    gn, fg, hx, part, grads, nrm,
):
    clear_ends(grads, 2)

    @pl.when(pl.program_id(0) == 0)
    def _():
        hx[...] = jnp.zeros_like(hx)

    for c in range(STEP):
        nrm[c] = nrm_in[c].astype(F32)
        local = slice(c * LANES, (c + 1) * LANES)
        second = a[:, local].astype(F32)
        span = jnp.exp(-float(BLOCK) * r_e[:, local])
        first = w_e[:, local] * b[:, local] + span * second
        states = jnp.concatenate([first, second], 1).astype(BF16)
        carried = stacked(dot(lrw[c, 0], by_group(states)))
        modal = gm[c].astype(F32)
        product = back[c] + carried + skip[:, local] * modal
        grads[c, 0, 8:136, :] = product * v[c]
        grads[c, 1, 8:136, :] = product * k[c]
        gains = gain[:, local]
        taps = [filt[j, 0:1, local] for j in range(21)]
        part[:, local] = (gn0[c, 0:8, :] + taken(grads, c, (1, 2), taps, 0, 8)).astype(BF16)
        gain_grad = jnp.zeros((8, LANES), F32)
        for r in range(0, LANES, 32):
            total = gn0[c, 8 + r : 40 + r, :] + taken(grads, c, (1, 2), taps, 8 + r, 32)
            gn[c, r : r + 32, :] = total
            xhat = x[r : r + 32, local].astype(F32) * inv[8 + r : 40 + r, :]
            both = total * xhat
            gain_grad = gain_grad + jnp.sum(both.reshape(4, 8, LANES), axis=0)
            hx[r : r + 32, :] += both * gains
        gain_grad = jnp.sum(gain_grad, axis=0, keepdims=True)
        rows = tap_gradients(grads, nrm, c, 2) + [gain_grad, jnp.zeros((1, LANES), F32)]
        fg[:, local] = jnp.concatenate(rows, 0)


def final_kernel(
    gn, g0, g1, g2, fg0, fg, hx, part, x, x_last, inv, gain, gain_all, out, cg, mean
):
    channels = x_last.shape[1]
    step = pl.program_id(0)

    @pl.when(step == 0)
    def _():
        def add(i, total):
            lanes = pl.ds(pl.multiple_of(i * LANES, LANES), LANES)
            xhat = x_last[8:16, lanes].astype(F32) * inv[128:136, :]
            return total + part[:, lanes].astype(F32) * gain_all[:, lanes] * xhat

        extra = lax.fori_loop(
            0, channels // LANES, add, jnp.zeros((8, LANES), F32), unroll=4
        )
        total = jnp.concatenate([hx[:120], hx[120:] + extra], 0)
        total = jnp.sum(total, axis=1, keepdims=True) * (1.0 / channels)
        mean[...] = jnp.broadcast_to(total, mean.shape)

    for c in range(STEP):
        local = slice(c * LANES, (c + 1) * LANES)
        lanes = pl.ds(pl.multiple_of((step * STEP + c) * LANES, LANES), LANES)
        arrived = joined((g0, g1, g2), local)
        extra = part[:, lanes].astype(F32)
        own = gn[c]
        own = jnp.concatenate([own[:120], own[120:] + extra], 0)
        xhat = x[:, local].astype(F32) * inv[8:136, :]
        result = arrived + inv[8:136, :] * (own * gain[:, local] - xhat * mean[...])
        out[:, local] = result.astype(BF16)
        fixed = jnp.sum(extra * xhat[120:], axis=0, keepdims=True)
        sources = [fg0[i : i + 1, local] for i in range(7)]
        sources += [fg[i : i + 1, local] for i in range(14)]
        sources += [fg[14:15, local] + fixed, fg0[7:8, local]]
        for i, source in enumerate(sources):
            cg[i, 0:1, local] = source


def modes_kernel(a, b, e, f, r_e, w_e, by_lag, lr, w, residue_out, rate_out):
    groups = lr.shape[1]
    chunks = e.shape[1] // LANES

    def chunk(i, total):
        lanes = pl.ds(pl.multiple_of(i * LANES, LANES), LANES)
        rate = r_e[:, lanes]
        weight = w_e[:, lanes]
        span = jnp.exp(-float(BLOCK) * rate)
        state0 = e[:, lanes]
        state1 = f[0:16, lanes] + span * state0
        adjoint1 = a[:, lanes].astype(F32)
        adjoint0 = weight * b[16:32, lanes] + span * adjoint1
        one = (state0 * b[0:16, lanes] + state1 * b[16:32, lanes]) * jnp.exp(-rate)
        two = weight * (state0 * b[32:48, lanes] + state1 * b[48:64, lanes])
        two = two + adjoint0 * f[32:48, lanes] + adjoint1 * f[48:64, lanes]
        two = two + BLOCK * span * (adjoint0 * state0 + adjoint1 * state1)
        both = jnp.concatenate([one, two], 0)
        high = both.astype(BF16)
        low = (both - high.astype(F32)).astype(BF16)
        shape = (LANES, groups)
        hot = (iota(shape, 1) == i * 8 + iota(shape, 0) // 16).astype(BF16)
        return total + dot(jnp.concatenate([high, low], 0), hot)

    totals = lax.fori_loop(0, chunks, chunk, jnp.zeros((64, groups), F32), unroll=8)
    totals = totals[:32] + totals[32:]
    lag = iota((LANES, groups), 0).astype(F32)
    lags = by_lag[...].T
    for m in range(16):
        rate = jnp.exp(lr[m : m + 1, :])
        terms = jnp.exp(-rate * lag) * lags
        first = jnp.sum(terms, axis=0, keepdims=True)
        second = jnp.sum(terms * lag, axis=0, keepdims=True) * jnp.exp(rate)
        residue_out[m : m + 1, :] = first + totals[m : m + 1, :]
        decay = w[m : m + 1, :] * second + totals[16 + m : 17 + m, :]
        rate_out[m : m + 1, :] = decay * (-jnp.exp(-rate) * rate)


def levels_of(count):
    levels = []
    stride = 1
    while stride < count:
        size = 2 if stride == 1 else min(4, count // stride)
        levels.append((stride, size))
        stride *= size
    return levels


def after(value, *others):
    return lax.optimization_barrier((value, *others))[0]


def shard_numbers(rows):
    count = lax.axis_size("seq")
    shard = lax.axis_index("seq")
    found = {"even": shard % 2 == 0}
    stride, size = levels_of(count)[-1]
    digit = (shard // stride) % size
    for h in range(1, size):
        found["onward", h] = digit + h < size
        found["later", h] = jnp.where(h <= digit, 0.0, 1.0)
    for reverse in (False, True):
        low = 0
        for number, (stride, size) in enumerate(levels_of(count)):
            digit = (shard // stride) % size
            place = size - 1 - digit if reverse else digit
            found[reverse, number, "own"] = (rows * stride * (size - 1 - place)).astype(F32)
            if number > 1:
                found[reverse, number, "low"] = (rows * low).astype(F32)
            found[reverse, number, "place"] = (rows * stride * place).astype(F32)
            for h in range(1, size):
                found[reverse, number, "earlier", h] = jnp.where(h <= place, 1.0, 0.0)
                away = rows * stride * ((h - 1 - place) % size)
                found[reverse, number, "away", h] = away.astype(F32)
            if number:
                low = low + place * stride
    return found


class Prefix:
    def __init__(self, local, rate, rows, reverse, column):
        self.count = lax.axis_size("seq")
        self.local, self.rate, self.rows, self.reverse = local, rate, rows, reverse
        self.column = column
        self.value = local
        self.levels = levels_of(self.count)
        self.above = 0.0

    def get(self, *name):
        return self.column((self.reverse,) + name)

    def mine(self, value):
        half = value.shape[1] // 2
        return jnp.where(self.column("even"), value[:, :half], value[:, half:])

    def send(self, number):
        stride, size = self.levels[number]
        last = stride * size == self.count
        sign = -1 if self.reverse else 1
        self.got = []
        for h in range(1, size):
            pairs = []
            for i in range(self.count):
                there = (i // stride) % size + sign * h
                if last and not 0 <= there < size:
                    continue
                pairs.append((i, i + (there % size - (i // stride) % size) * stride))
            self.got.append(lax.ppermute(self.value, "seq", pairs))

    def join(self, number, *others):
        stride, size = self.levels[number]
        last = stride * size == self.count
        rate = self.rate if number == 0 else self.mine(self.rate)
        span = float(self.rows * stride)
        got = self.got
        if others:
            got = [after(item, *others) for item in got]
        own = self.value.astype(F32)
        group = own * jnp.exp(-rate * self.get(number, "own"))
        before = jnp.zeros_like(own)
        for h in range(1, size):
            item = got[h - 1].astype(F32)
            earlier = self.get(number, "earlier", h)
            before = before + item * (earlier * jnp.exp(-rate * (span * (h - 1))))
            if not last:
                group = group + item * jnp.exp(-rate * self.get(number, "away", h))
        if number == 0:
            self.near = before
            group = self.mine(group)
        else:
            if number > 1:
                before = before * jnp.exp(-rate * self.get(number, "low"))
            self.above = self.above + before
        self.value = group.astype(self.local.dtype)


def send_both(ahead, behind):
    stride, size = ahead.levels[-1]
    got = []
    for h in range(1, size):
        pairs = []
        for i in range(ahead.count):
            digit = (i // stride) % size
            pairs.append((i, i + ((digit + h) % size - digit) * stride))
        value = jnp.where(ahead.column(("onward", h)), ahead.value, behind.value.astype(F32))
        got.append(lax.ppermute(value, "seq", pairs))
    return got


def join_both(ahead, behind, got):
    number = len(ahead.levels) - 1
    stride, size = ahead.levels[-1]
    rate = ahead.mine(ahead.rate)
    span = float(ahead.rows * stride)
    states = adjoints = 0.0
    for h in range(1, size):
        item = got[h - 1]
        near = jnp.exp(-rate * (span * (h - 1)))
        states = states + item * (ahead.get(number, "earlier", h) * near)
        near = jnp.exp(-rate * (span * (size - h - 1)))
        adjoints = adjoints + item * (ahead.column(("later", h)) * near)
    states = ahead.above + states * jnp.exp(-rate * ahead.get(number, "low"))
    adjoints = behind.above + adjoints * jnp.exp(-rate * behind.get(number, "low"))
    mine = jnp.concatenate([states, adjoints], 0)
    other = lax.ppermute(mine, "seq", [(i, i ^ 1) for i in range(ahead.count)])
    even = ahead.column("even")
    low, high = jnp.where(even, mine, other), jnp.where(even, other, mine)
    above = jnp.concatenate([low, high], 1)
    states = ahead.near + above[:16] * jnp.exp(-ahead.rate * ahead.get(0, "place"))
    adjoints = behind.near + above[16:] * jnp.exp(-ahead.rate * behind.get(0, "place"))
    return states, adjoints.astype(BF16)


def on_device(section_input, sent_grad, norm_gain, short_filter, log_rate, residue, skip_gain):
    x = section_input[0]
    rows, channels = x.shape
    groups = log_rate.shape[2]
    chunks = channels // LANES
    sections = lax.axis_size("section")
    count = lax.axis_size("seq")
    filt, gain, skip = short_filter.reshape(-1, 1, channels), norm_gain, skip_gain
    names, numbers = zip(*shard_numbers(rows).items())
    lr, w, *numbers = lax.optimization_barrier((log_rate[0], residue[0], *numbers))
    column = dict(zip(names, numbers)).__getitem__

    ring = [(i, (i - 1) % sections) for i in range(sections)]
    cuts = (0, rows * 2 // 8, rows * 5 // 8, rows)
    g = [
        lax.ppermute(sent_grad[0, low:high], "section", ring)
        for low, high in zip(cuts[:-1], cuts[1:])
    ]
    arrived = [(item, (item.shape[0], WIDE), lambda i: (0, i)) for item in g]
    halo = lax.ppermute(x[rows - 8 :], "seq", [(i, i + 1) for i in range(count - 1)])

    full = lambda i: (0, 0)
    lane = lambda i: (0, i)
    block = lambda i: (i, 0, 0)
    cube = (STEP, LANES, LANES)
    tall = (STEP, LANES + 8, LANES)
    normal = (STEP, LANES + 16, LANES)
    grid = (chunks // STEP,)
    table_step = min(TABLE_STEP, chunks)
    table_groups = 8 * table_step
    lc, lrw, kk, r_e, w_e = call(
        table_kernel,
        (chunks // table_step,),
        [(lr, (16, table_groups), lane), (w, (16, table_groups), lane)],
        [
            (
                (chunks, 3, LANES, LANES),
                BF16,
                (table_step, 3, LANES, LANES),
                lambda i: (i, 0, 0, 0),
            ),
            (
                (chunks, 2, BLOCK, LANES),
                BF16,
                (table_step, 2, BLOCK, LANES),
                lambda i: (i, 0, 0, 0),
            ),
            ((2, groups, LANES), F32, (2, table_groups, LANES), lambda i: (0, i, 0)),
            ((16, channels), F32, (16, table_step * LANES), lane),
            ((16, channels), F32, (16, table_step * LANES), lane),
        ],
        micros=0,
        name="tables",
    )
    wide16 = (16, WIDE)
    nrm, q, k, v, p, inside, inv, s, f = call(
        features_kernel,
        grid,
        [
            (x, (rows, channels), full),
            (after(halo, g[0]), (8, channels), full),
            (gain, (1, WIDE), lane),
            (filt, (21, 1, WIDE), lambda i: (0, 0, i)),
            (lc, (STEP, 2, LANES, LANES), lambda i: (i, 0, 0, 0)),
            (kk, (1, 8 * STEP, LANES), lambda i: (0, i, 0)),
            (r_e, wide16, lane),
        ],
        [
            ((chunks, LANES + 16, LANES), BF16, normal, block),
            ((chunks, LANES, LANES), F32, cube, block),
            ((chunks, LANES, LANES), F32, cube, block),
            ((chunks, LANES, LANES), F32, cube, block),
            ((2, chunks, LANES, LANES), BF16, (2,) + cube, lambda i: (0, i, 0, 0)),
            ((chunks, LANES, LANES), F32, cube, block),
            ((LANES + 8, LANES), F32, (LANES + 8, LANES), full),
            ((16, channels), F32, wide16, lane),
            ((64, channels), F32, (64, WIDE), lane),
        ],
        scratch=[pltpu.VMEM((LANES + 8, LANES), F32), pltpu.VMEM(tall, F32)],
        micros=0,
        name="features",
    )
    ahead = Prefix(after(s, g[1]), r_e, rows, False, column)
    ahead.send(0)
    ahead.join(0)
    ahead.send(1)
    q_late = after(q, ahead.value)
    gm, a_local, b = call(
        adjoint_kernel,
        grid,
        [
            *arrived,
            (q_late, cube, block),
            (lc, (STEP, 1, LANES, LANES), lambda i: (i, 2, 0, 0)),
            (w_e, wide16, lane),
            (r_e, wide16, lane),
        ],
        [
            ((chunks, LANES, LANES), BF16, cube, block),
            ((16, channels), BF16, wide16, lane),
            ((64, channels), F32, (64, WIDE), lane),
        ],
        micros=0,
        name="adjoint",
    )
    (back,) = call(
        backward_kernel,
        grid,
        [
            (after(gm, a_local), cube, block),
            (kk, (1, 8 * STEP, LANES), lambda i: (1, i, 0)),
        ],
        [((chunks, LANES, LANES), F32, cube, block)],
        micros=0,
        name="backward",
    )
    ahead.got = [after(item, back) for item in ahead.got]
    behind = Prefix(after(a_local, *ahead.got), r_e, rows, True, column)
    behind.send(0)
    ahead.join(1)
    behind.join(0)
    behind.send(1)
    behind.join(1)
    got = send_both(ahead, behind)
    (by_lag,) = call(
        lags_kernel,
        grid,
        [
            (after(p, behind.value, ahead.value), (2,) + cube, lambda i: (0, i, 0, 0)),
            (gm, cube, block),
        ],
        [((groups, LANES), F32, (8 * STEP, LANES), lambda i: (i, 0))],
        micros=6,
        name="lags",
    )
    e, a = join_both(ahead, behind, [after(item, by_lag) for item in got])
    block_out, gn0, fg0 = call(
        output_kernel,
        grid,
        [
            (inside, cube, block),
            (lrw, (STEP, 1, BLOCK, LANES), lambda i: (i, 0, 0, 0)),
            (e, wide16, lane),
            (f, wide16, lane),
            (r_e, wide16, lane),
            (q, cube, block),
            (p, (2,) + cube, lambda i: (0, i, 0, 0)),
            (x, (rows, WIDE), lane),
            (skip, (1, WIDE), lane),
            *arrived,
            (nrm, normal, block),
            (filt, (21, 1, WIDE), lambda i: (0, 0, i)),
        ],
        [
            ((rows, channels), BF16, (rows, WIDE), lane),
            ((chunks, LANES + 8, LANES), F32, tall, block),
            ((8, channels), F32, (8, WIDE), lane),
        ],
        scratch=[pltpu.VMEM((STEP, 1, LANES + 16, LANES), F32), pltpu.VMEM(normal, F32)],
        micros=8,
        name="output",
    )
    gn, fg, hx, part = call(
        mixer_kernel,
        grid,
        [
            (back, cube, block),
            (lrw, (STEP, 1, BLOCK, LANES), lambda i: (i, 1, 0, 0)),
            (a, wide16, lane),
            (b, wide16, lambda i: (1, i)),
            (w_e, wide16, lane),
            (r_e, wide16, lane),
            (gm, cube, block),
            (k, cube, block),
            (v, cube, block),
            (gn0, tall, block),
            (nrm, normal, block),
            (filt, (21, 1, WIDE), lambda i: (0, 0, i)),
            (skip, (1, WIDE), lane),
            (gain, (1, WIDE), lane),
            (x, (rows, WIDE), lane),
            (inv, (LANES + 8, LANES), full),
        ],
        [
            ((chunks, LANES, LANES), F32, cube, block),
            ((16, channels), F32, wide16, lane),
            ((LANES, LANES), F32, (LANES, LANES), full),
            ((8, channels), BF16, (8, WIDE), lane),
        ],
        scratch=[pltpu.VMEM((STEP, 2, LANES + 16, LANES), F32), pltpu.VMEM(normal, F32)],
        micros=10,
        name="mixer",
    )
    part = lax.ppermute(part, "seq", [(i + 1, i) for i in range(count - 1)])
    whole = lambda value: (value, value.shape, lambda i: (0,) * value.ndim)
    residue_grads, rate_grads = call(
        modes_kernel,
        (1,),
        [whole(value) for value in (a, b, e, f, r_e, w_e, by_lag, lr, w)],
        [((16, groups), F32, (16, groups), full)] * 2,
        micros=3,
        name="modes",
    )
    input_grad, channel_grads = call(
        final_kernel,
        grid,
        [
            (gn, cube, block),
            *arrived,
            (fg0, (8, WIDE), lane),
            (fg, wide16, lane),
            (hx, (LANES, LANES), full),
            (part, (8, channels), full),
            (x, (rows, WIDE), lane),
            (x, (16, channels), lambda i: (rows // 16 - 1, 0)),
            (inv, (LANES + 8, LANES), full),
            (gain, (1, WIDE), lane),
            (gain, (1, channels), full),
        ],
        [
            ((rows, channels), BF16, (rows, WIDE), lane),
            ((23, 1, channels), F32, (23, 1, WIDE), lambda i: (0, 0, i)),
        ],
        scratch=[pltpu.VMEM((LANES, LANES), F32)],
        micros=4,
        name="final",
    )
    return (
        block_out[None],
        input_grad[None],
        channel_grads.reshape(1, 1, 23, channels),
        residue_grads[None, None],
        rate_grads[None, None],
    )


def solution(mesh):
    placed = (
        P("section", "seq", None),
        P("section", "seq", None),
        P("section", None),
        P("section", None, None),
        P("section", None, None),
        P("section", None, None),
        P("section", None),
    )
    return jax.shard_map(
        on_device,
        mesh=mesh,
        in_specs=placed,
        out_specs=(
            P("section", "seq", None),
            P("section", "seq", None),
            P("section", "seq", None, None),
            P("section", "seq", None, None),
            P("section", "seq", None, None),
        ),
        check_vma=False,
    )
```

```python
import jax
import jax.numpy as jnp
from jax import lax
from jax.experimental import pallas as pl
from jax.experimental.pallas import tpu as pltpu
from jax.sharding import PartitionSpec as P

EPSILON = 1e-06
F32 = jnp.float32
BF16 = jnp.bfloat16
LANES = 128
STEP = 16
WIDE = STEP * LANES
BLOCK = 64
TABLE_STEP = 16
VMEM_LIMIT = 26 * 1024 * 1024


def iota(shape, axis):
    return lax.broadcasted_iota(jnp.int32, shape, axis)


def dot(a, b):
    return jnp.dot(a, b, preferred_element_type=F32)


def call(kernel, grid, ins, outs, scratch=(), micros=1.0, name=None):
    total = sum(a.size * a.dtype.itemsize for a, _, _ in ins)
    for shape, dtype, _, _ in outs:
        size = jnp.dtype(dtype).itemsize
        for n in shape:
            size *= n
        total += size
    return pl.pallas_call(
        kernel,
        grid=grid,
        in_specs=[pl.BlockSpec(b, m) for _, b, m in ins],
        out_specs=[pl.BlockSpec(b, m) for _, _, b, m in outs],
        out_shape=[jax.ShapeDtypeStruct(s, d) for s, d, _, _ in outs],
        scratch_shapes=list(scratch),
        compiler_params=pltpu.CompilerParams(
            dimension_semantics=("arbitrary",) * len(grid), vmem_limit_bytes=VMEM_LIMIT
        ),
        cost_estimate=pl.CostEstimate(
            flops=int(micros * 1.0e9),
            bytes_accessed=int(total) if micros else 0,
            transcendentals=0,
        ),
        name=name,
    )(*[a for a, _, _ in ins])


def lane_group(shape):
    return (iota(shape, 1) % LANES) // 16


def by_group(rows):
    own = lane_group(rows.shape)
    zero = jnp.zeros_like(rows)
    return jnp.concatenate([jnp.where(own == g, rows, zero) for g in range(8)], 0)


def own_group(rows):
    own = lane_group((16, rows.shape[1]))
    kept = rows[:16]
    for g in range(1, 8):
        kept = jnp.where(own == g, rows[16 * g : 16 * g + 16], kept)
    return kept


def side_by_side(rows):
    return jnp.concatenate([rows[:BLOCK], rows[BLOCK:]], 1)


def joined(parts, lanes):
    return jnp.concatenate([part[:, lanes] for part in parts], 0).astype(F32)


def stacked(rows):
    return jnp.concatenate([rows[:, :LANES], rows[:, LANES:]], 0)


def table_kernel(lr, w, lc, lrw, kk, r_e, w_e):
    shape = (16, LANES)
    first = iota(shape, 1) < BLOCK
    token = (iota(shape, 1) % BLOCK).astype(F32)
    own = lane_group(shape)

    def split(value):
        high = value.astype(BF16).astype(F32)
        return jnp.where(first, high, value - high)

    for c in range(lc.shape[0]):
        parts = [[] for _ in range(4)]
        rate_lanes = weight_lanes = None
        for g in range(8):
            at = c * 8 + g
            rate = jnp.broadcast_to(jnp.exp(lr[:, at : at + 1]), shape)
            weight = jnp.broadcast_to(w[:, at : at + 1], shape)
            end = jnp.exp(-rate * (BLOCK - 1.0 - token))
            start = jnp.exp(-rate * token)
            decay = jnp.exp(-rate)
            parts[0].append(split(end))
            parts[1].append(split((BLOCK - 1.0 - token) * end))
            parts[2].append(jnp.where(first, 1.0, token + 1.0) * start)
            parts[3].append(decay * jnp.where(first, weight * start, end))
            for i, value in enumerate((end, start)):
                row = jnp.sum(weight * value, axis=0, keepdims=True)
                kk[i, at : at + 1, :] = jnp.where(first[:1], row, 0.0)
            if g == 0:
                rate_lanes, weight_lanes = rate, weight
            else:
                rate_lanes = jnp.where(own == g, rate, rate_lanes)
                weight_lanes = jnp.where(own == g, weight, weight_lanes)
        for i in range(3):
            lc[c, i] = jnp.concatenate(parts[i], 0).astype(BF16)
        turned = jnp.concatenate(parts[3], 0).T.astype(BF16)
        lrw[c, 0] = turned[:BLOCK]
        lrw[c, 1] = turned[BLOCK:]
        lanes = slice(c * LANES, (c + 1) * LANES)
        r_e[:, lanes] = rate_lanes
        w_e[:, lanes] = weight_lanes


def features_kernel(
    x, xh, gain, filt, lc, kk, r_e, nrm_out, q, k, v, p, inside, inv_out, s, f, inv, nrm
):
    channels = x.shape[1]
    step = pl.program_id(0)

    @pl.when(step == 0)
    def _():
        def add(i, carry):
            own, halo = carry
            lanes = pl.ds(pl.multiple_of(i * LANES, LANES), LANES)
            a = x[:, lanes].astype(F32)
            b = xh[:, lanes].astype(F32)
            return own + a * a, halo + b * b

        own, halo = lax.fori_loop(
            0,
            channels // LANES,
            add,
            (jnp.zeros((LANES, LANES), F32), jnp.zeros((8, LANES), F32)),
            unroll=4,
        )
        for rows, total in ((slice(0, 8), halo), (slice(8, 136), own)):
            mean = jnp.sum(total, axis=1, keepdims=True) * (1.0 / channels)
            inverse = lax.rsqrt(mean + EPSILON)
            inv[rows, :] = jnp.broadcast_to(inverse, total.shape)
        inv_out[...] = inv[...]

    for c in range(STEP):
        local = slice(c * LANES, (c + 1) * LANES)
        lanes = pl.ds(pl.multiple_of((step * STEP + c) * LANES, LANES), LANES)
        gains = gain[:, local]
        own = x[:, lanes].astype(F32) * inv[8:136, :]
        own = (own * gains).astype(BF16)
        nrm_out[c, 16:144, :] = own
        nrm[c, 8:136, :] = own.astype(F32)
        halo = xh[:, lanes].astype(F32) * inv[0:8, :]
        halo = (halo * gains).astype(BF16).astype(F32)
        nrm_out[c, 0:16, :] = jnp.concatenate([jnp.zeros_like(halo), halo], 0).astype(BF16)
        nrm[c, 0:8, :] = halo
        taps = [filt[j, 0:1, local] for j in range(21)]
        for r in range(0, LANES, 32):
            total = [jnp.zeros((32, LANES), F32) for _ in range(3)]
            for j in range(7):
                rows = nrm[c, 8 + r - j : 40 + r - j, :]
                for i in range(3):
                    total[i] = total[i] + taps[i * 7 + j] * rows
            q[c, r : r + 32, :] = total[0]
            k[c, r : r + 32, :] = total[1]
            v[c, r : r + 32, :] = total[2]
            product = total[1] * total[2]
            high = product.astype(BF16)
            p[0, c, r : r + 32, :] = high
            p[1, c, r : r + 32, :] = (product - high.astype(F32)).astype(BF16)
    for c in range(STEP):
        local = slice(c * LANES, (c + 1) * LANES)
        high, low = side_by_side(p[0, c]), side_by_side(p[1, c])
        table = lc[c].reshape(2 * LANES, LANES)
        sums = dot(
            jnp.concatenate([table, table], 1), jnp.concatenate([high, high, low, low], 0)
        )
        ends, ramps = own_group(sums[:LANES]), own_group(sums[LANES:])
        span = jnp.exp(-float(BLOCK) * r_e[:, local])
        s[:, local] = span * ends[:, :LANES] + ends[:, LANES:]
        f[0:32, local] = stacked(ends)
        f[32:64, local] = stacked(ramps)
        inside[c] = forward_blocks(p[0, c], kk[0, c * 8 : c * 8 + 8, :])


def forward_blocks(p, kernel):
    first = iota((BLOCK, LANES), 1) < BLOCK
    tiles = []
    for g in range(0, 8, 2):
        even, odd = (jnp.broadcast_to(kernel[i : i + 1], (BLOCK, LANES)) for i in (g, g + 1))
        even = pltpu.roll(even, BLOCK + 1, 1, stride=1, stride_axis=0)
        odd = pltpu.roll(odd, 1, 1, stride=1, stride_axis=0)
        tiles.append(jnp.where(first, even, odd).astype(BF16))
    return stacked(dot(jnp.concatenate(tiles, 1), by_group(side_by_side(p))))


def taken(grads, c, streams, taps, first, rows):
    total = None
    for i, stream in enumerate(streams):
        for j in range(7):
            term = taps[stream * 7 + j] * grads[c, i, first + j : first + j + rows, :]
            total = term if total is None else total + term
    return total


def tap_gradients(grads, nrm, c, count):
    sums = [jnp.zeros((8, LANES), F32) for _ in range(7 * count)]
    for r in range(0, LANES, 32):
        items = [grads[c, i, 8 + r : 40 + r, :] for i in range(count)]
        for j in range(7):
            rows = nrm[c, 16 + r - j : 48 + r - j, :]
            for i in range(count):
                term = (items[i] * rows).reshape(4, 8, LANES)
                sums[i * 7 + j] = sums[i * 7 + j] + jnp.sum(term, axis=0)
    return [jnp.sum(item, axis=0, keepdims=True) for item in sums]


def clear_ends(grads, count):
    @pl.when(pl.program_id(0) == 0)
    def _():
        for i in range(count):
            grads[:, i, 0:8, :] = jnp.zeros((STEP, 8, LANES), F32)
            grads[:, i, 136:144, :] = jnp.zeros((STEP, 8, LANES), F32)


def output_kernel(
    inside, lrw, e, f, r_e, q, p, x, skip, g0, g1, g2, nrm_in, filt, out, gn, fg, grads, nrm
):
    clear_ends(grads, 1)
    for c in range(STEP):
        nrm[c] = nrm_in[c].astype(F32)
        local = slice(c * LANES, (c + 1) * LANES)
        state = e[:, local]
        second = f[:, local] + jnp.exp(-float(BLOCK) * r_e[:, local]) * state
        states = jnp.concatenate([state, second], 1).astype(BF16)
        carried = stacked(dot(lrw[c, 0], by_group(states)))
        product = p[0, c].astype(F32) + p[1, c].astype(F32)
        modal = inside[c] + carried + skip[:, local] * product
        query = q[c]
        arrived = joined((g0, g1, g2), local)
        out[:, local] = (x[:, local].astype(F32) + query * modal).astype(BF16)
        grads[c, 0, 8:136, :] = arrived * modal
        skip_grad = jnp.sum(arrived * query * product, axis=0, keepdims=True)
        taps = [filt[j, 0:1, local] for j in range(7)]
        gn[c, 0:8, :] = taken(grads, c, (0,), taps, 0, 8)
        for r in range(8, 136, 32):
            gn[c, r : r + 32, :] = taken(grads, c, (0,), taps, r, 32)
        fg[:, local] = jnp.concatenate(tap_gradients(grads, nrm, c, 1) + [skip_grad], 0)


def adjoint_kernel(g0, g1, g2, q, lc, w_e, r_e, gm, a, b):
    for c in range(STEP):
        local = slice(c * LANES, (c + 1) * LANES)
        grad = (joined((g0, g1, g2), local) * q[c]).astype(BF16)
        gm[c] = grad
        sides = side_by_side(grad)
        none = jnp.zeros_like(sides)
        sides = jnp.concatenate(
            [jnp.concatenate([sides, none], 1), jnp.concatenate([none, sides], 1)], 0
        )
        sums = own_group(dot(lc[c, 0], sides))
        starts, ramps = sums[:, : 2 * LANES], sums[:, 2 * LANES :]
        span = jnp.exp(-float(BLOCK) * r_e[:, local])
        first = w_e[:, local] * (starts[:, :LANES] + span * starts[:, LANES:])
        a[:, local] = first.astype(BF16)
        b[0:32, local] = stacked(starts)
        b[32:64, local] = stacked(ramps)


def lags_kernel(p, gm, by_lag):
    first = iota((1, LANES), 1) < BLOCK
    shape = (BLOCK, LANES)
    causal = iota(shape, 1) % BLOCK + iota(shape, 0) >= BLOCK - 1
    both = iota((LANES, LANES), 0) + iota((LANES, LANES), 1)
    same = iota((LANES, LANES), 0) // BLOCK == iota((LANES, LANES), 1) // BLOCK
    flip = (same & (both % BLOCK == BLOCK - 1)).astype(BF16)
    for c in range(STEP):
        grads = by_group(side_by_side(gm[c]))
        sides = jnp.concatenate([side_by_side(p[0, c]), side_by_side(p[1, c])], 0)
        sides = dot(flip, sides).astype(BF16)
        crossed = lax.dot_general(
            sides, grads, (((1,), (1,)), ((), ())), preferred_element_type=F32
        )
        crossed = crossed[:BLOCK] + crossed[BLOCK:]
        for g in range(0, 8, 2):
            tile = jnp.where(causal, crossed[:, g * BLOCK : (g + 2) * BLOCK], 0.0)
            tile = pltpu.roll(tile, BLOCK + 1, 1, stride=1, stride_axis=0)
            tile = jnp.sum(tile, axis=0, keepdims=True)
            at = c * 8 + g
            by_lag[at : at + 1, :] = jnp.where(first, tile, 0.0)
            by_lag[at + 1 : at + 2, :] = jnp.where(first, pltpu.roll(tile, BLOCK, 1), 0.0)


def backward_kernel(gm, kk, back):
    first = iota((BLOCK, LANES), 1) < BLOCK
    for c in range(STEP):
        tiles = []
        for g in range(0, 8, 2):
            even, odd = (
                jnp.broadcast_to(kk[0, c * 8 + i : c * 8 + i + 1, :], (BLOCK, LANES))
                for i in (g, g + 1)
            )
            even = pltpu.roll(even, 0, 1, stride=1, stride_axis=0)
            odd = pltpu.roll(odd, BLOCK, 1, stride=1, stride_axis=0)
            tiles.append(jnp.where(first, even, odd).astype(BF16))
        back[c] = stacked(dot(jnp.concatenate(tiles, 1), by_group(side_by_side(gm[c]))))


def mixer_kernel(
    back, lrw, a, b, w_e, r_e, gm, k, v, gn0, nrm_in, filt, skip, gain, x, inv,
    gn, fg, hx, part, grads, nrm,
):
    clear_ends(grads, 2)

    @pl.when(pl.program_id(0) == 0)
    def _():
        hx[...] = jnp.zeros_like(hx)

    for c in range(STEP):
        nrm[c] = nrm_in[c].astype(F32)
        local = slice(c * LANES, (c + 1) * LANES)
        second = a[:, local].astype(F32)
        span = jnp.exp(-float(BLOCK) * r_e[:, local])
        first = w_e[:, local] * b[:, local] + span * second
        states = jnp.concatenate([first, second], 1).astype(BF16)
        carried = stacked(dot(lrw[c, 0], by_group(states)))
        modal = gm[c].astype(F32)
        product = back[c] + carried + skip[:, local] * modal
        grads[c, 0, 8:136, :] = product * v[c]
        grads[c, 1, 8:136, :] = product * k[c]
        gains = gain[:, local]
        taps = [filt[j, 0:1, local] for j in range(21)]
        part[:, local] = (gn0[c, 0:8, :] + taken(grads, c, (1, 2), taps, 0, 8)).astype(BF16)
        gain_grad = jnp.zeros((8, LANES), F32)
        for r in range(0, LANES, 32):
            total = gn0[c, 8 + r : 40 + r, :] + taken(grads, c, (1, 2), taps, 8 + r, 32)
            gn[c, r : r + 32, :] = total
            xhat = x[r : r + 32, local].astype(F32) * inv[8 + r : 40 + r, :]
            both = total * xhat
            gain_grad = gain_grad + jnp.sum(both.reshape(4, 8, LANES), axis=0)
            hx[r : r + 32, :] += both * gains
        gain_grad = jnp.sum(gain_grad, axis=0, keepdims=True)
        rows = tap_gradients(grads, nrm, c, 2) + [gain_grad, jnp.zeros((1, LANES), F32)]
        fg[:, local] = jnp.concatenate(rows, 0)


def final_kernel(
    gn, g0, g1, g2, fg0, fg, hx, part, x, x_last, inv, gain, gain_all, out, cg, mean
):
    channels = x_last.shape[1]
    step = pl.program_id(0)

    @pl.when(step == 0)
    def _():
        def add(i, total):
            lanes = pl.ds(pl.multiple_of(i * LANES, LANES), LANES)
            xhat = x_last[8:16, lanes].astype(F32) * inv[128:136, :]
            return total + part[:, lanes].astype(F32) * gain_all[:, lanes] * xhat

        extra = lax.fori_loop(
            0, channels // LANES, add, jnp.zeros((8, LANES), F32), unroll=4
        )
        total = jnp.concatenate([hx[:120], hx[120:] + extra], 0)
        total = jnp.sum(total, axis=1, keepdims=True) * (1.0 / channels)
        mean[...] = jnp.broadcast_to(total, mean.shape)

    for c in range(STEP):
        local = slice(c * LANES, (c + 1) * LANES)
        lanes = pl.ds(pl.multiple_of((step * STEP + c) * LANES, LANES), LANES)
        arrived = joined((g0, g1, g2), local)
        extra = part[:, lanes].astype(F32)
        own = gn[c]
        own = jnp.concatenate([own[:120], own[120:] + extra], 0)
        xhat = x[:, local].astype(F32) * inv[8:136, :]
        result = arrived + inv[8:136, :] * (own * gain[:, local] - xhat * mean[...])
        out[:, local] = result.astype(BF16)
        fixed = jnp.sum(extra * xhat[120:], axis=0, keepdims=True)
        sources = [fg0[i : i + 1, local] for i in range(7)]
        sources += [fg[i : i + 1, local] for i in range(14)]
        sources += [fg[14:15, local] + fixed, fg0[7:8, local]]
        for i, source in enumerate(sources):
            cg[i, 0:1, local] = source


def modes_kernel(a, b, e, f, r_e, w_e, by_lag, lr, w, residue_out, rate_out):
    groups = lr.shape[1]
    chunks = e.shape[1] // LANES

    def chunk(i, total):
        lanes = pl.ds(pl.multiple_of(i * LANES, LANES), LANES)
        rate = r_e[:, lanes]
        weight = w_e[:, lanes]
        span = jnp.exp(-float(BLOCK) * rate)
        state0 = e[:, lanes]
        state1 = f[0:16, lanes] + span * state0
        adjoint1 = a[:, lanes].astype(F32)
        adjoint0 = weight * b[16:32, lanes] + span * adjoint1
        one = (state0 * b[0:16, lanes] + state1 * b[16:32, lanes]) * jnp.exp(-rate)
        two = weight * (state0 * b[32:48, lanes] + state1 * b[48:64, lanes])
        two = two + adjoint0 * f[32:48, lanes] + adjoint1 * f[48:64, lanes]
        two = two + BLOCK * span * (adjoint0 * state0 + adjoint1 * state1)
        both = jnp.concatenate([one, two], 0)
        high = both.astype(BF16)
        low = (both - high.astype(F32)).astype(BF16)
        shape = (LANES, groups)
        hot = (iota(shape, 1) == i * 8 + iota(shape, 0) // 16).astype(BF16)
        return total + dot(jnp.concatenate([high, low], 0), hot)

    totals = lax.fori_loop(0, chunks, chunk, jnp.zeros((64, groups), F32), unroll=8)
    totals = totals[:32] + totals[32:]
    lag = iota((LANES, groups), 0).astype(F32)
    lags = by_lag[...].T
    for m in range(16):
        rate = jnp.exp(lr[m : m + 1, :])
        terms = jnp.exp(-rate * lag) * lags
        first = jnp.sum(terms, axis=0, keepdims=True)
        second = jnp.sum(terms * lag, axis=0, keepdims=True) * jnp.exp(rate)
        residue_out[m : m + 1, :] = first + totals[m : m + 1, :]
        decay = w[m : m + 1, :] * second + totals[16 + m : 17 + m, :]
        rate_out[m : m + 1, :] = decay * (-jnp.exp(-rate) * rate)


def levels_of(count):
    levels = []
    stride = 1
    while stride < count:
        size = 2 if stride == 1 else min(4, count // stride)
        levels.append((stride, size))
        stride *= size
    return levels


def after(value, *others):
    return lax.optimization_barrier((value, *others))[0]


def shard_numbers(rows):
    count = lax.axis_size("seq")
    shard = lax.axis_index("seq")
    found = {"even": shard % 2 == 0}
    stride, size = levels_of(count)[-1]
    digit = (shard // stride) % size
    for h in range(1, size):
        found["onward", h] = digit + h < size
        found["later", h] = jnp.where(h <= digit, 0.0, 1.0)
    for reverse in (False, True):
        low = 0
        for number, (stride, size) in enumerate(levels_of(count)):
            digit = (shard // stride) % size
            place = size - 1 - digit if reverse else digit
            found[reverse, number, "own"] = (rows * stride * (size - 1 - place)).astype(F32)
            if number > 1:
                found[reverse, number, "low"] = (rows * low).astype(F32)
            found[reverse, number, "place"] = (rows * stride * place).astype(F32)
            for h in range(1, size):
                found[reverse, number, "earlier", h] = jnp.where(h <= place, 1.0, 0.0)
                away = rows * stride * ((h - 1 - place) % size)
                found[reverse, number, "away", h] = away.astype(F32)
            if number:
                low = low + place * stride
    return found


class Prefix:
    def __init__(self, local, rate, rows, reverse, column):
        self.count = lax.axis_size("seq")
        self.local, self.rate, self.rows, self.reverse = local, rate, rows, reverse
        self.column = column
        self.value = local
        self.levels = levels_of(self.count)
        self.above = 0.0

    def get(self, *name):
        return self.column((self.reverse,) + name)

    def mine(self, value):
        half = value.shape[1] // 2
        return jnp.where(self.column("even"), value[:, :half], value[:, half:])

    def send(self, number):
        stride, size = self.levels[number]
        last = stride * size == self.count
        sign = -1 if self.reverse else 1
        self.got = []
        for h in range(1, size):
            pairs = []
            for i in range(self.count):
                there = (i // stride) % size + sign * h
                if last and not 0 <= there < size:
                    continue
                pairs.append((i, i + (there % size - (i // stride) % size) * stride))
            self.got.append(lax.ppermute(self.value, "seq", pairs))

    def join(self, number, *others):
        stride, size = self.levels[number]
        last = stride * size == self.count
        rate = self.rate if number == 0 else self.mine(self.rate)
        span = float(self.rows * stride)
        got = self.got
        if others:
            got = [after(item, *others) for item in got]
        own = self.value.astype(F32)
        group = own * jnp.exp(-rate * self.get(number, "own"))
        before = jnp.zeros_like(own)
        for h in range(1, size):
            item = got[h - 1].astype(F32)
            earlier = self.get(number, "earlier", h)
            before = before + item * (earlier * jnp.exp(-rate * (span * (h - 1))))
            if not last:
                group = group + item * jnp.exp(-rate * self.get(number, "away", h))
        if number == 0:
            self.near = before
            group = self.mine(group)
        else:
            if number > 1:
                before = before * jnp.exp(-rate * self.get(number, "low"))
            self.above = self.above + before
        self.value = group.astype(self.local.dtype)


def send_both(ahead, behind):
    stride, size = ahead.levels[-1]
    got = []
    for h in range(1, size):
        pairs = []
        for i in range(ahead.count):
            digit = (i // stride) % size
            pairs.append((i, i + ((digit + h) % size - digit) * stride))
        value = jnp.where(ahead.column(("onward", h)), ahead.value, behind.value.astype(F32))
        got.append(lax.ppermute(value, "seq", pairs))
    return got


def join_both(ahead, behind, got):
    number = len(ahead.levels) - 1
    stride, size = ahead.levels[-1]
    rate = ahead.mine(ahead.rate)
    span = float(ahead.rows * stride)
    states = adjoints = 0.0
    for h in range(1, size):
        item = got[h - 1]
        near = jnp.exp(-rate * (span * (h - 1)))
        states = states + item * (ahead.get(number, "earlier", h) * near)
        near = jnp.exp(-rate * (span * (size - h - 1)))
        adjoints = adjoints + item * (ahead.column(("later", h)) * near)
    states = ahead.above + states * jnp.exp(-rate * ahead.get(number, "low"))
    adjoints = behind.above + adjoints * jnp.exp(-rate * behind.get(number, "low"))
    mine = jnp.concatenate([states, adjoints], 0)
    other = lax.ppermute(mine, "seq", [(i, i ^ 1) for i in range(ahead.count)])
    even = ahead.column("even")
    low, high = jnp.where(even, mine, other), jnp.where(even, other, mine)
    above = jnp.concatenate([low, high], 1)
    states = ahead.near + above[:16] * jnp.exp(-ahead.rate * ahead.get(0, "place"))
    adjoints = behind.near + above[16:] * jnp.exp(-ahead.rate * behind.get(0, "place"))
    return states, adjoints.astype(BF16)


def on_device(section_input, sent_grad, norm_gain, short_filter, log_rate, residue, skip_gain):
    x = section_input[0]
    rows, channels = x.shape
    groups = log_rate.shape[2]
    chunks = channels // LANES
    sections = lax.axis_size("section")
    count = lax.axis_size("seq")
    filt, gain, skip = short_filter.reshape(-1, 1, channels), norm_gain, skip_gain
    names, numbers = zip(*shard_numbers(rows).items())
    lr, w, *numbers = lax.optimization_barrier((log_rate[0], residue[0], *numbers))
    column = dict(zip(names, numbers)).__getitem__

    ring = [(i, (i - 1) % sections) for i in range(sections)]
    cuts = (0, rows * 2 // 8, rows * 5 // 8, rows)
    g = [
        lax.ppermute(sent_grad[0, low:high], "section", ring)
        for low, high in zip(cuts[:-1], cuts[1:])
    ]
    arrived = [(item, (item.shape[0], WIDE), lambda i: (0, i)) for item in g]
    halo = lax.ppermute(x[rows - 8 :], "seq", [(i, i + 1) for i in range(count - 1)])

    full = lambda i: (0, 0)
    lane = lambda i: (0, i)
    block = lambda i: (i, 0, 0)
    cube = (STEP, LANES, LANES)
    tall = (STEP, LANES + 8, LANES)
    normal = (STEP, LANES + 16, LANES)
    grid = (chunks // STEP,)
    table_step = min(TABLE_STEP, chunks)
    table_groups = 8 * table_step
    lc, lrw, kk, r_e, w_e = call(
        table_kernel,
        (chunks // table_step,),
        [(lr, (16, table_groups), lane), (w, (16, table_groups), lane)],
        [
            (
                (chunks, 3, LANES, LANES),
                BF16,
                (table_step, 3, LANES, LANES),
                lambda i: (i, 0, 0, 0),
            ),
            (
                (chunks, 2, BLOCK, LANES),
                BF16,
                (table_step, 2, BLOCK, LANES),
                lambda i: (i, 0, 0, 0),
            ),
            ((2, groups, LANES), F32, (2, table_groups, LANES), lambda i: (0, i, 0)),
            ((16, channels), F32, (16, table_step * LANES), lane),
            ((16, channels), F32, (16, table_step * LANES), lane),
        ],
        micros=0,
        name="tables",
    )
    wide16 = (16, WIDE)
    nrm, q, k, v, p, inside, inv, s, f = call(
        features_kernel,
        grid,
        [
            (x, (rows, channels), full),
            (after(halo, g[0]), (8, channels), full),
            (gain, (1, WIDE), lane),
            (filt, (21, 1, WIDE), lambda i: (0, 0, i)),
            (lc, (STEP, 2, LANES, LANES), lambda i: (i, 0, 0, 0)),
            (kk, (1, 8 * STEP, LANES), lambda i: (0, i, 0)),
            (r_e, wide16, lane),
        ],
        [
            ((chunks, LANES + 16, LANES), BF16, normal, block),
            ((chunks, LANES, LANES), F32, cube, block),
            ((chunks, LANES, LANES), F32, cube, block),
            ((chunks, LANES, LANES), F32, cube, block),
            ((2, chunks, LANES, LANES), BF16, (2,) + cube, lambda i: (0, i, 0, 0)),
            ((chunks, LANES, LANES), F32, cube, block),
            ((LANES + 8, LANES), F32, (LANES + 8, LANES), full),
            ((16, channels), F32, wide16, lane),
            ((64, channels), F32, (64, WIDE), lane),
        ],
        scratch=[pltpu.VMEM((LANES + 8, LANES), F32), pltpu.VMEM(tall, F32)],
        micros=0,
        name="features",
    )
    ahead = Prefix(after(s, g[1]), r_e, rows, False, column)
    ahead.send(0)
    ahead.join(0)
    ahead.send(1)
    q_late = after(q, ahead.value)
    gm, a_local, b = call(
        adjoint_kernel,
        grid,
        [
            *arrived,
            (q_late, cube, block),
            (lc, (STEP, 1, LANES, LANES), lambda i: (i, 2, 0, 0)),
            (w_e, wide16, lane),
            (r_e, wide16, lane),
        ],
        [
            ((chunks, LANES, LANES), BF16, cube, block),
            ((16, channels), BF16, wide16, lane),
            ((64, channels), F32, (64, WIDE), lane),
        ],
        micros=0,
        name="adjoint",
    )
    (back,) = call(
        backward_kernel,
        grid,
        [
            (after(gm, a_local), cube, block),
            (kk, (1, 8 * STEP, LANES), lambda i: (1, i, 0)),
        ],
        [((chunks, LANES, LANES), F32, cube, block)],
        micros=0,
        name="backward",
    )
    ahead.got = [after(item, back) for item in ahead.got]
    behind = Prefix(after(a_local, *ahead.got), r_e, rows, True, column)
    behind.send(0)
    ahead.join(1)
    behind.join(0)
    behind.send(1)
    behind.join(1)
    got = send_both(ahead, behind)
    (by_lag,) = call(
        lags_kernel,
        grid,
        [
            (after(p, behind.value, ahead.value), (2,) + cube, lambda i: (0, i, 0, 0)),
            (gm, cube, block),
        ],
        [((groups, LANES), F32, (8 * STEP, LANES), lambda i: (i, 0))],
        micros=6,
        name="lags",
    )
    e, a = join_both(ahead, behind, [after(item, by_lag) for item in got])
    block_out, gn0, fg0 = call(
        output_kernel,
        grid,
        [
            (inside, cube, block),
            (lrw, (STEP, 1, BLOCK, LANES), lambda i: (i, 0, 0, 0)),
            (e, wide16, lane),
            (f, wide16, lane),
            (r_e, wide16, lane),
            (q, cube, block),
            (p, (2,) + cube, lambda i: (0, i, 0, 0)),
            (x, (rows, WIDE), lane),
            (skip, (1, WIDE), lane),
            *arrived,
            (nrm, normal, block),
            (filt, (21, 1, WIDE), lambda i: (0, 0, i)),
        ],
        [
            ((rows, channels), BF16, (rows, WIDE), lane),
            ((chunks, LANES + 8, LANES), F32, tall, block),
            ((8, channels), F32, (8, WIDE), lane),
        ],
        scratch=[pltpu.VMEM((STEP, 1, LANES + 16, LANES), F32), pltpu.VMEM(normal, F32)],
        micros=8,
        name="output",
    )
    gn, fg, hx, part = call(
        mixer_kernel,
        grid,
        [
            (back, cube, block),
            (lrw, (STEP, 1, BLOCK, LANES), lambda i: (i, 1, 0, 0)),
            (a, wide16, lane),
            (b, wide16, lambda i: (1, i)),
            (w_e, wide16, lane),
            (r_e, wide16, lane),
            (gm, cube, block),
            (k, cube, block),
            (v, cube, block),
            (gn0, tall, block),
            (nrm, normal, block),
            (filt, (21, 1, WIDE), lambda i: (0, 0, i)),
            (skip, (1, WIDE), lane),
            (gain, (1, WIDE), lane),
            (x, (rows, WIDE), lane),
            (inv, (LANES + 8, LANES), full),
        ],
        [
            ((chunks, LANES, LANES), F32, cube, block),
            ((16, channels), F32, wide16, lane),
            ((LANES, LANES), F32, (LANES, LANES), full),
            ((8, channels), BF16, (8, WIDE), lane),
        ],
        scratch=[pltpu.VMEM((STEP, 2, LANES + 16, LANES), F32), pltpu.VMEM(normal, F32)],
        micros=10,
        name="mixer",
    )
    part = lax.ppermute(part, "seq", [(i + 1, i) for i in range(count - 1)])
    whole = lambda value: (value, value.shape, lambda i: (0,) * value.ndim)
    residue_grads, rate_grads = call(
        modes_kernel,
        (1,),
        [whole(value) for value in (a, b, e, f, r_e, w_e, by_lag, lr, w)],
        [((16, groups), F32, (16, groups), full)] * 2,
        micros=3,
        name="modes",
    )
    input_grad, channel_grads = call(
        final_kernel,
        grid,
        [
            (gn, cube, block),
            *arrived,
            (fg0, (8, WIDE), lane),
            (fg, wide16, lane),
            (hx, (LANES, LANES), full),
            (part, (8, channels), full),
            (x, (rows, WIDE), lane),
            (x, (16, channels), lambda i: (rows // 16 - 1, 0)),
            (inv, (LANES + 8, LANES), full),
            (gain, (1, WIDE), lane),
            (gain, (1, channels), full),
        ],
        [
            ((rows, channels), BF16, (rows, WIDE), lane),
            ((23, 1, channels), F32, (23, 1, WIDE), lambda i: (0, 0, i)),
        ],
        scratch=[pltpu.VMEM((LANES, LANES), F32)],
        micros=4,
        name="final",
    )
    return (
        block_out[None],
        input_grad[None],
        channel_grads.reshape(1, 1, 23, channels),
        residue_grads[None, None],
        rate_grads[None, None],
    )


def solution(mesh):
    placed = (
        P("section", "seq", None),
        P("section", "seq", None),
        P("section", None),
        P("section", None, None),
        P("section", None, None),
        P("section", None, None),
        P("section", None),
    )
    return jax.shard_map(
        on_device,
        mesh=mesh,
        in_specs=placed,
        out_specs=(
            P("section", "seq", None),
            P("section", "seq", None),
            P("section", "seq", None, None),
            P("section", "seq", None, None),
            P("section", "seq", None, None),
        ),
        check_vma=False,
    )
```
